32 devices in a mesh: dp: 8 (over y, x, core), tp: 4 (over z).
Axes of the slice: x: 2, y: 2, z: 4, core: 2. Of those that a mesh axis runs over, the one named last changes fastest.
Arguments:
- hidden: bfloat16 [8192, 6144], P('dp', 'tp'), may hold values from -6 to 6
- norm_gain: float32 [6144], P('tp'), may hold values from 0.1 to 1.9
- kv_weight: bfloat16 [6144, 1536], P('tp'), may hold values from -0.078125 to 0.078125
- owners: int32 [8192, 1], P('dp'), may hold values from 0 to 7; in each aligned block of 1024 rows (0 to 1023, 1024 to 2047, ...) at most 256 rows name the same one
- offsets: int32 [8192], P('dp'), may hold values from 0 to 4095
Outputs:
- kv_slots: bfloat16 [1536, 16384], P('tp', 'dp')
The draws below stay inside these ranges and needn't reach their ends.
Inputs may be any that keep to these rules, and one draw needn't show every extreme that they name: `owners`: among the 1024 rows of one group no owner is named more than 256 times, a bound that some block reaches.
All inputs are finite; a program needn't handle non-finite values.
Results may differ from the reference program's by a relative error of at most 0.0049.
Values may be sent and summed in bfloat16 or wider, within the bound.
A program may use at most 64 MiB of HBM per device.

```python
import math
from functools import partial
import jax
import jax.numpy as jnp
import numpy as np
from jax import lax

D_WIN = 6144
KV_HEADS = 6
HEAD = 128
KV_COLS = 1536
ROWS_DEV = 1024
CAP = 256
TOKENS = 8192
SLOTS = 16384
N_DP = 8


def set_ends(values, own_key, smallest, largest):
    index_at = [jax.random.randint(jax.random.fold_in(own_key, axis), (), 0, length) for axis, length in enumerate(values.shape)]
    longest = values.shape.index(max(values.shape))
    beside = index_at[:longest] + [(index_at[longest] + 1) % values.shape[longest]] + index_at[longest + 1:]
    return values.at[tuple(index_at)].set(smallest).at[tuple(beside)].set(largest)


def levels(key, extent, pieces, least, top_value):
    factor_of, own = 1.0, jax.random.fold_in(key, 6)
    for dim, shards_of in pieces:
        steps = jnp.exp(jax.random.uniform(jax.random.fold_in(own, dim), (shards_of,), jnp.float32, least / len(pieces), top_value / len(pieces)))
        factor_of = factor_of * jnp.repeat(steps, extent[dim] // shards_of).reshape([-1 if axis == dim else 1 for axis in range(len(extent))])
    return factor_of


def shared_out(stream_key, own, number, rows, count, top, reach, skew):
    order = jax.random.permutation(stream_key, count)
    crowded, usual = portions_of(count, rows * top, reach, skew, True), portions_of(count, rows * top, reach, skew, False)
    places = jnp.arange(count)

    def named(sizes, turn):
        used = int((sizes > 0).sum())
        fixed = max(1, used // 4)
        passed = fixed + (places - fixed + turn * (used - fixed)) % max(1, count - fixed)
        return jnp.zeros((count,), jnp.int32).at[order[jnp.where(places < fixed, places, passed)]].set(jnp.asarray(sizes, jnp.int32))

    sizes = jnp.where(number % 4 == 0, named(crowded, number // 4), named(usual, number - number // 4 - 1))
    mixed = jax.random.permutation(jax.random.fold_in(own, 3), count)
    source_of, receiver = mixed[0:count // 2 * 2:2], mixed[1:count // 2 * 2:2]
    room = jnp.minimum(sizes[source_of] - 1, reach - sizes[receiver]) // 2
    room = jnp.where((source_of == order[0]) | (receiver == order[0]) | (sizes[receiver] == 0), 0, jnp.maximum(room, 0))
    passed = jax.random.randint(jax.random.fold_in(own, 4), (count // 2,), 0, 1 << 20) % (room + 1)
    sizes = sizes.at[source_of].add(-passed).at[receiver].add(passed)
    labels = jnp.searchsorted(jnp.cumsum(sizes), jnp.arange(rows * top), side="right").astype(jnp.int32)
    table = labels.reshape(top, rows).T
    table = table[jax.random.permutation(jax.random.fold_in(own, 1), rows)]
    turn = jax.random.randint(jax.random.fold_in(own, 2), (rows, 1), 0, top)
    return jnp.take_along_axis(table, (jnp.arange(top)[None, :] + turn) % top, axis=1)


def portions_of(count, total, reach, skew, full):
    weights = [(1 << 20) // math.isqrt(standing ** skew) + 1 for standing in range(1, count + 1)]
    largest = reach if full else min(reach, max(-(-total // count), total * weights[0] // sum(weights)))
    least = 1 if total - largest >= count - 1 else 0
    given, surplus = [largest] + [least] * (count - 1), total - largest - least * (count - 1)
    while surplus > 0:
        movable = [i for i in range(1, count) if given[i] < largest] or [i for i in range(1, count) if given[i] < reach]
        mass, left = sum([weights[i] for i in movable]), surplus
        for i in movable:
            more = min(reach - given[i], max(1, left * weights[i] // mass), surplus)
            given[i] = given[i] + more
            surplus = surplus - more
    return np.array(given)


def noise(key, extent, spread, bound, pieces=(), kind=jnp.bfloat16):
    values = spread * jax.random.normal(key, extent, jnp.float32)
    if pieces:
        values = values * levels(key, extent, pieces, -0.22, 0.18)
    return jnp.clip(values, -bound, bound).astype(kind)


def setup_inputs(seed: int = 0) -> dict:
    splits = jax.random.split(jax.random.key(seed), 6)
    hidden = noise(splits[0], (TOKENS, D_WIN), 1.0, 6.0, ((0, 8), (1, 4)))
    norm_gain = jnp.clip(1.0 + 0.18 * jax.random.normal(splits[1], (D_WIN,), jnp.float32), 0.1, 1.9)
    kv_weight = noise(splits[2], (D_WIN, KV_COLS), D_WIN ** -0.5, 0.078125, ((0, 4),))
    owners_keys = jax.random.split(jax.random.fold_in(splits[3], 1), TOKENS // ROWS_DEV)
    owners_turns = jax.random.permutation(jax.random.fold_in(splits[3], 3), TOKENS // ROWS_DEV)
    owners = jax.vmap(lambda own, number: shared_out(jax.random.fold_in(splits[3], 2), own, number, ROWS_DEV, N_DP, 1, CAP, 2))(owners_keys, owners_turns).reshape((TOKENS, 1))
    offsets = set_ends(jax.random.randint(splits[4], (TOKENS,), 0, 4096), jax.random.fold_in(splits[4], 1), 0, 4095).astype(jnp.int32)
    return dict(hidden=hidden, norm_gain=norm_gain, kv_weight=kv_weight, owners=owners, offsets=offsets)


EPSILON = 1e-05
ROPE_BASE = 500000.0

def rotate_keys(projected, positions, first_block):
    col_count, row_count = projected.shape
    half_dim = HEAD // 2
    block_count = col_count // HEAD
    exponent = jnp.arange(half_dim, dtype=jnp.float32) * (2.0 / HEAD)
    inverse = ROPE_BASE ** (-exponent)
    angles = inverse[:, None] * positions.astype(jnp.float32)[None, :]
    cosine = jnp.cos(angles)
    sine = jnp.sin(angles)
    blocks = projected.reshape(block_count, 2, half_dim, row_count)
    first_half = blocks[:, 0]
    second_half = blocks[:, 1]
    turned = jnp.stack([first_half * cosine - second_half * sine, second_half * cosine + first_half * sine], axis=1)
    is_key = first_block + jnp.arange(block_count, dtype=jnp.int32) < KV_HEADS
    return jnp.where(is_key[:, None, None, None], turned, blocks).reshape(col_count, row_count)

def rank_within(destination, peers):
    onehot = (destination[:, None] == jnp.arange(peers, dtype=jnp.int32)[None, :]).astype(jnp.int32)
    before = jnp.cumsum(onehot, axis=0) - onehot
    return lax.optimization_barrier(jnp.sum(before * onehot, axis=1)).astype(jnp.int32)

def reference(hidden, norm_gain, kv_weight, owners, offsets):
    widened = hidden.astype(jnp.float32)
    total = lax.optimization_barrier(jnp.sum(widened * widened, axis=1))
    normed = (widened * lax.rsqrt(total / D_WIN + EPSILON)[:, None] * norm_gain[None, :]).astype(jnp.bfloat16)
    projected = lax.dot_general(kv_weight, normed, (((0,), (1,)), ((), ())), preferred_element_type=jnp.float32)
    rotated = rotate_keys(projected, offsets, 0).astype(jnp.bfloat16)
    destination = owners[:, 0].reshape(N_DP, ROWS_DEV)
    within = jax.vmap(partial(rank_within, peers=N_DP))(destination)
    source = jnp.arange(N_DP, dtype=jnp.int32)[:, None]
    target = (destination * (N_DP * CAP) + source * CAP + within).reshape(-1).astype(jnp.int32)
    result = jnp.zeros((KV_COLS, SLOTS), jnp.bfloat16)
    return result.at[:, target].set(rotated)
```

```python
import functools

import jax
import jax.numpy as jnp
from jax import lax
from jax.experimental import pallas as pl
from jax.experimental.pallas import tpu as pltpu
from jax.sharding import PartitionSpec as P

HEAD = 128
EPSILON = 1e-05
ROPE_BASE = 500000.0
MESH = pl.DeviceIdType.MESH
F32 = jnp.float32
BF16 = jnp.bfloat16
EXACT = lax.Precision.HIGHEST


def to_columns(rows):
    weight = jnp.full((rows.shape[0], 128), 0.125, F32)
    return lax.dot_general(
        rows, weight, (((0,), (0,)), ((), ())), precision=EXACT, preferred_element_type=F32
    )


def kernel(
    tp, dp, chunks, cap, key_heads, direct,
    h_ref, g_ref, w_ref, owner_ref, offset_ref, inverse_ref, out_ref,
    hg, squares, part, sendbuf, from_left, from_right, totals, places, cosine, sine, scale, outgoing,
    total_send, total_recv, send_sem, left_recv, right_recv, out_send, out_recv, own_sem,
):
    z = lax.axis_index("tp")
    group = lax.axis_index("dp")
    rows, features = h_ref.shape
    width = chunks * HEAD
    slots = dp * cap
    edge = (z == 0) | (z == tp - 1)

    barrier = pltpu.get_barrier_semaphore()
    for r in range(1, tp):
        pl.semaphore_signal(barrier, inc=1, device_id={"tp": lax.rem(z + r, tp)}, device_id_type=MESH)
    if direct:
        for r in range(1, dp):
            pl.semaphore_signal(barrier, inc=1, device_id={"dp": lax.rem(group + r, dp)}, device_id_type=MESH)

    @pl.loop(0, rows // 16)
    def _(step):
        at = pl.ds(pl.multiple_of(step * 16, 16), 16)
        wide = h_ref[at, :].astype(F32)
        hg[at, :] = (wide * g_ref[...]).astype(BF16)
        wide = wide * wide
        total = wide[:, 0:128]
        for lane in range(128, features, 128):
            total = total + wide[:, lane:lane + 128]
        squares[at, :] = total

    pl.semaphore_wait(barrier, tp - 1 + (dp - 1 if direct else 0))

    def to_right(index):
        return pltpu.make_async_remote_copy(
            src_ref=sendbuf.at[index], dst_ref=from_left.at[index],
            send_sem=send_sem.at[index], recv_sem=left_recv.at[index],
            device_id={"tp": jnp.minimum(z + 1, tp - 1)}, device_id_type=MESH,
        )

    def to_left(index):
        return pltpu.make_async_remote_copy(
            src_ref=sendbuf.at[index], dst_ref=from_right.at[index],
            send_sem=send_sem.at[index], recv_sem=right_recv.at[index],
            device_id={"tp": jnp.maximum(z - 1, 0)}, device_id_type=MESH,
        )

    tile = rows // 2

    @pl.loop(0, tp)
    def _(turn):
        dest = jnp.where(z == tp - 1, turn, tp - 1 - turn)
        columns = pl.ds(pl.multiple_of(dest * width, HEAD), width)

        @pl.loop(0, rows // tile)
        def _(step):
            at = pl.ds(pl.multiple_of(step * tile, tile), tile)
            term = jnp.dot(hg[at, :], w_ref[:, columns], preferred_element_type=F32)
            for k in range(chunks):
                piece = term[:, k * HEAD:(k + 1) * HEAD]
                part[dest * chunks + k, at, :] = piece
                sendbuf[dest * chunks + k, at, :] = piece.astype(BF16)

        for k in range(chunks):
            @pl.when((turn == 0) & (z == 0))
            def _():
                to_right((tp - 1) * chunks + k).start()

            @pl.when((turn == 0) & (z == tp - 1))
            def _():
                to_left(k).start()

    totals[z] = lax.dot_general(
        jnp.ones((8, 128), F32), squares[...], (((1,), (1,)), ((), ())),
        precision=EXACT, preferred_element_type=F32,
    )
    total_copies = []
    for r in range(1, tp):
        copy = pltpu.make_async_remote_copy(
            src_ref=totals.at[z], dst_ref=totals.at[z],
            send_sem=total_send.at[r], recv_sem=total_recv.at[r],
            device_id={"tp": lax.rem(z + r, tp)}, device_id_type=MESH,
        )
        copy.start()
        total_copies.append(copy)

    owner = to_columns(jnp.broadcast_to(owner_ref[...].astype(F32), (8, rows)))
    lane = lax.broadcasted_iota(jnp.int32, (1, 128), 1).astype(F32)
    named = jnp.where(owner == lane, 1.0, 0.0)
    earlier = jnp.where(
        lax.broadcasted_iota(jnp.int32, (rows, rows), 0) > lax.broadcasted_iota(jnp.int32, (rows, rows), 1),
        1.0, 0.0,
    ).astype(BF16)
    before = jnp.dot(earlier, named.astype(BF16), preferred_element_type=F32)
    rank = jnp.sum(before * named, axis=1, keepdims=True)
    slot = owner[:, 0:1] * cap + rank
    for first in range(0, slots, 256):
        here = (lax.broadcasted_iota(jnp.int32, (1, 256), 1) + first).astype(F32)
        places[:, first:first + 256] = jnp.where(slot == here, 1.0, 0.0).astype(BF16)
    offset = to_columns(jnp.broadcast_to(offset_ref[...].astype(F32), (8, rows)))
    angle = offset * inverse_ref[...]
    cosine[...] = jnp.cos(angle)
    sine[...] = jnp.where(lane < HEAD // 2, -1.0, 1.0) * jnp.sin(angle)

    for r in range(1, tp):
        total_copies[r - 1].wait()
    total = to_columns(totals[...].reshape(tp * 8, rows))
    scale[...] = lax.rsqrt(total / (features * tp) + EPSILON)

    def out_copy(k, r, sender, target):
        return pltpu.make_async_remote_copy(
            src_ref=outgoing.at[k, :, pl.ds(pl.multiple_of(target * cap, cap), cap)],
            dst_ref=out_ref.at[pl.ds(pl.multiple_of(k * HEAD, HEAD), HEAD), pl.ds(pl.multiple_of(sender * cap, cap), cap)],
            send_sem=out_send.at[k, r], recv_sem=out_recv.at[k, r],
            device_id={"dp": target}, device_id_type=MESH,
        )

    def own_copy(k):
        rows_at = pl.ds(pl.multiple_of(k * HEAD, HEAD), HEAD)
        if not direct:
            return pltpu.make_async_copy(outgoing.at[k], out_ref.at[rows_at, :], own_sem.at[k])
        at = pl.ds(pl.multiple_of(group * cap, cap), cap)
        return pltpu.make_async_copy(outgoing.at[k, :, at], out_ref.at[rows_at, at], own_sem.at[k])

    last_turn = jnp.where(edge, tp - 2, tp - 1)

    @pl.loop(0, tp * chunks)
    def _(step):
        turn = step // chunks
        k = lax.rem(step, chunks)
        right = tp - 1 - turn
        left = turn
        right_index = right * chunks + k
        left_index = left * chunks + k

        @pl.when((right > z) & (z > 0))
        def _():
            to_right(right_index).wait_recv()
            sendbuf[right_index] = (part[right_index] + from_left[right_index].astype(F32)).astype(BF16)
            to_right(right_index).start()

        @pl.when((left < z) & (z < tp - 1))
        def _():
            to_left(left_index).wait_recv()
            sendbuf[left_index] = (part[left_index] + from_right[left_index].astype(F32)).astype(BF16)
            to_left(left_index).start()

        @pl.when((right > 0) & (z == 0) & (turn > 0))
        def _():
            to_right(right_index + chunks).wait_send()
            to_right(right_index).start()

        @pl.when((left < tp - 1) & (z == tp - 1) & (turn > 0))
        def _():
            to_left(left_index - chunks).wait_send()
            to_left(left_index).start()

        @pl.when(turn == last_turn)
        def _():
            index = z * chunks + k

            @pl.when(z > 0)
            def _():
                to_right(index).wait_recv()
                part[index] = part[index] + from_left[index].astype(F32)

            @pl.when(z < tp - 1)
            def _():
                to_left(index).wait_recv()
                part[index] = part[index] + from_right[index].astype(F32)

            value = part[index] * scale[...]
            turned = value * cosine[...] + pltpu.roll(value, HEAD // 2, 1) * sine[...]
            rotated = jnp.where(index < key_heads, turned, value).astype(BF16)
            outgoing[k] = lax.dot_general(
                rotated, places[...], (((0,), (0,)), ((), ())), preferred_element_type=F32
            ).astype(BF16)
            if direct:
                for r in range(1, dp):
                    out_copy(k, r, group, lax.rem(group + r, dp)).start()
            own_copy(k).start()

    last_dest = jnp.where(z == 0, 1, tp - 2)

    @pl.loop(0, tp * chunks)
    def _(index):
        dest = index // chunks
        open_send = jnp.logical_not(edge) | (dest == last_dest)

        @pl.when((dest > z) & open_send)
        def _():
            to_right(index).wait_send()

        @pl.when((dest < z) & open_send)
        def _():
            to_left(index).wait_send()

    for k in range(chunks):
        own_copy(k).wait()
        if direct:
            for r in range(1, dp):
                out_copy(k, r, group, lax.rem(group + r, dp)).wait_send()
                out_copy(k, r, lax.rem(group + dp - r, dp), group).wait_recv()


def per_device(hidden, norm_gain, kv_weight, owners, offsets):
    dp, tp = lax.axis_size("dp"), lax.axis_size("tp")
    rows, features = hidden.shape
    cap = 2 * rows // dp
    columns = kv_weight.shape[1]
    share = columns // tp
    chunks = share // HEAD
    direct = cap % 128 == 0
    exponent = (jnp.arange(HEAD, dtype=jnp.int32) % (HEAD // 2)).astype(F32) * (2.0 / HEAD)
    inverse = (ROPE_BASE ** (-exponent))[None, :]
    vmem = pl.BlockSpec(memory_space=pltpu.VMEM)
    pieces = tp * chunks
    dma = pltpu.SemaphoreType.DMA
    result = pl.pallas_call(
        functools.partial(kernel, tp, dp, chunks, cap, columns // (2 * HEAD), direct),
        out_shape=jax.ShapeDtypeStruct((share, dp * cap), BF16),
        in_specs=[vmem] * 6,
        out_specs=pl.BlockSpec(memory_space=pl.ANY),
        scratch_shapes=[
            pltpu.VMEM((rows, features), BF16),
            pltpu.VMEM((rows, 128), F32),
            pltpu.VMEM((pieces, rows, HEAD), F32),
            pltpu.VMEM((pieces, rows, HEAD), BF16),
            pltpu.VMEM((pieces, rows, HEAD), BF16),
            pltpu.VMEM((pieces, rows, HEAD), BF16),
            pltpu.VMEM((tp, 8, rows), F32),
            pltpu.VMEM((rows, dp * cap), BF16),
            pltpu.VMEM((rows, HEAD), F32),
            pltpu.VMEM((rows, HEAD), F32),
            pltpu.VMEM((rows, HEAD), F32),
            pltpu.VMEM((chunks, HEAD, dp * cap), BF16),
            dma((tp,)), dma((tp,)), dma((pieces,)), dma((pieces,)), dma((pieces,)),
            dma((chunks, dp)), dma((chunks, dp)), dma((chunks,)),
        ],
        compiler_params=pltpu.CompilerParams(
            collective_id=0, has_side_effects=True, vmem_limit_bytes=56 * 1024 * 1024
        ),
    )(hidden, norm_gain[None, :], kv_weight, owners.reshape(1, rows), offsets.reshape(1, rows), inverse)
    if direct:
        return result
    received = lax.all_to_all(
        result.reshape(share, dp, cap), "dp", split_axis=1, concat_axis=1, tiled=True
    )
    return received.reshape(share, dp * cap)


def solution(mesh):
    in_specs = (P("dp", "tp"), P("tp"), P("tp", None), P("dp", None), P("dp"))
    out_specs = P("tp", "dp")
    return jax.shard_map(
        per_device, mesh=mesh, in_specs=in_specs, out_specs=out_specs, check_vma=False
    )
```

```python
import functools

import jax
import jax.numpy as jnp
import numpy as np
from jax import lax
from jax.experimental import pallas as pl
from jax.experimental.pallas import tpu as pltpu
from jax.sharding import PartitionSpec as P

HEAD = 128
EPSILON = 1e-05
ROPE_BASE = 500000.0
MESH = pl.DeviceIdType.MESH
BANDS = 4
F32 = jnp.float32
BF16 = jnp.bfloat16
EXACT = lax.Precision.HIGHEST


def to_columns(rows):
    weight = jnp.full((rows.shape[0], 128), 0.125, F32)
    return lax.dot_general(
        rows, weight, (((0,), (0,)), ((), ())), precision=EXACT, preferred_element_type=F32
    )


def kernel(
    tp, dp, chunks, cap, key_heads, direct,
    h_hbm, g_ref, w_hbm, owner_ref, offset_ref, inverse_ref, out_ref,
    h_ref, w_ref, hg, squares, part, sendbuf, from_left, from_right, totals, places, cosine, sine, scale, outgoing,
    total_send, total_recv, send_sem, left_recv, right_recv, out_send, out_recv, own_sem, h_sem, w_sem,
):
    z = lax.axis_index("tp")
    group = lax.axis_index("dp")
    rows, features = h_ref.shape
    width = chunks * HEAD
    slots = dp * cap
    edge = (z == 0) | (z == tp - 1)

    barrier = pltpu.get_barrier_semaphore()
    for r in range(1, tp):
        pl.semaphore_signal(barrier, inc=1, device_id={"tp": lax.rem(z + r, tp)}, device_id_type=MESH)
    if direct:
        for r in range(1, dp):
            pl.semaphore_signal(barrier, inc=1, device_id={"dp": lax.rem(group + r, dp)}, device_id_type=MESH)

    def h_copy(band):
        at = pl.ds(band * (rows // BANDS), rows // BANDS)
        return pltpu.make_async_copy(h_hbm.at[at, :], h_ref.at[at, :], h_sem.at[band])

    def w_copy(turn):
        dest = jnp.where(z == tp - 1, turn, tp - 1 - turn)
        at = pl.ds(pl.multiple_of(dest * width, HEAD), width)
        return pltpu.make_async_copy(w_hbm.at[:, at], w_ref.at[:, at], w_sem.at[turn])

    for band in range(BANDS):
        h_copy(band).start()
    for turn in range(tp):
        w_copy(turn).start()

    for band in range(BANDS):
        h_copy(band).wait()

        def scale_rows(step, carry, band=band):
            at = pl.ds(pl.multiple_of(band * (rows // BANDS) + step * 32, 32), 32)
            for lane in range(0, features, 128):
                gain = g_ref[lane // 128:lane // 128 + 1, :]
                hg[at, lane:lane + 128] = (h_ref[at, lane:lane + 128].astype(F32) * gain).astype(BF16)
            return carry

        lax.fori_loop(0, rows // BANDS // 32, scale_rows, 0, unroll=4)

    pl.semaphore_wait(barrier, tp - 1 + (dp - 1 if direct else 0))

    def to_right(index):
        return pltpu.make_async_remote_copy(
            src_ref=sendbuf.at[index], dst_ref=from_left.at[index],
            send_sem=send_sem.at[index], recv_sem=left_recv.at[index],
            device_id={"tp": jnp.minimum(z + 1, tp - 1)}, device_id_type=MESH,
        )

    def to_left(index):
        return pltpu.make_async_remote_copy(
            src_ref=sendbuf.at[index], dst_ref=from_right.at[index],
            send_sem=send_sem.at[index], recv_sem=right_recv.at[index],
            device_id={"tp": jnp.maximum(z - 1, 0)}, device_id_type=MESH,
        )

    tile = rows // 2
    ahead = min(2, chunks)

    @pl.loop(0, tp)
    def _(turn):
        dest = jnp.where(z == tp - 1, turn, tp - 1 - turn)
        columns = pl.ds(pl.multiple_of(dest * width, HEAD), width)
        w_copy(turn).wait()

        @pl.loop(0, rows // tile)
        def _(step):
            at = pl.ds(pl.multiple_of(step * tile, tile), tile)
            term = jnp.dot(hg[at, :], w_ref[:, columns], preferred_element_type=F32)
            for k in range(chunks):
                piece = term[:, k * HEAD:(k + 1) * HEAD]
                part[dest * chunks + k, at, :] = piece
                sendbuf[dest * chunks + k, at, :] = piece.astype(BF16)

        @pl.when((turn == 0) & (z == 0))
        def _():
            for n in range(ahead):
                to_right((tp - 1 - n // chunks) * chunks + n % chunks).start()

        @pl.when((turn == 0) & (z == tp - 1))
        def _():
            for n in range(ahead):
                to_left(n).start()

    def add_squares(step, carry):
        at = pl.ds(pl.multiple_of(step * 32, 32), 32)
        total = jnp.zeros((32, 128), F32)
        for lane in range(0, features, 128):
            wide = h_ref[at, lane:lane + 128].astype(F32)
            total = total + wide * wide
        squares[at, :] = total
        return carry

    lax.fori_loop(0, rows // 32, add_squares, 0, unroll=4)

    totals[z] = lax.dot_general(
        jnp.ones((8, 128), F32), squares[...], (((1,), (1,)), ((), ())),
        precision=EXACT, preferred_element_type=F32,
    )
    total_copies = []
    for r in range(1, tp):
        copy = pltpu.make_async_remote_copy(
            src_ref=totals.at[z], dst_ref=totals.at[z],
            send_sem=total_send.at[r], recv_sem=total_recv.at[r],
            device_id={"tp": lax.rem(z + r, tp)}, device_id_type=MESH,
        )
        copy.start()
        total_copies.append(copy)

    owner = to_columns(jnp.broadcast_to(owner_ref[...].astype(F32), (8, rows)))
    lane = lax.broadcasted_iota(jnp.int32, (1, 128), 1).astype(F32)
    named = jnp.where(owner == lane, 1.0, 0.0)
    earlier = jnp.where(
        lax.broadcasted_iota(jnp.int32, (rows, rows), 0) > lax.broadcasted_iota(jnp.int32, (rows, rows), 1),
        1.0, 0.0,
    ).astype(BF16)
    before = jnp.dot(earlier, named.astype(BF16), preferred_element_type=F32)
    rank = jnp.sum(before * named, axis=1, keepdims=True)
    slot = owner[:, 0:1] * cap + rank
    for first in range(0, slots, 256):
        here = (lax.broadcasted_iota(jnp.int32, (1, 256), 1) + first).astype(F32)
        places[:, first:first + 256] = jnp.where(slot == here, 1.0, 0.0).astype(BF16)
    offset = to_columns(jnp.broadcast_to(offset_ref[...].astype(F32), (8, rows)))
    angle = offset * inverse_ref[...]
    cosine[...] = jnp.cos(angle)
    sine[...] = jnp.where(lane < HEAD // 2, -1.0, 1.0) * jnp.sin(angle)

    for r in range(1, tp):
        total_copies[r - 1].wait()
    total = to_columns(totals[...].reshape(tp * 8, rows))
    scale[...] = lax.rsqrt(total / (features * tp) + EPSILON)

    def out_copy(k, r, sender, target):
        return pltpu.make_async_remote_copy(
            src_ref=outgoing.at[k, :, pl.ds(pl.multiple_of(target * cap, cap), cap)],
            dst_ref=out_ref.at[pl.ds(pl.multiple_of(k * HEAD, HEAD), HEAD), pl.ds(pl.multiple_of(sender * cap, cap), cap)],
            send_sem=out_send.at[k, r], recv_sem=out_recv.at[k, r],
            device_id={"dp": target}, device_id_type=MESH,
        )

    def own_copy(k):
        rows_at = pl.ds(pl.multiple_of(k * HEAD, HEAD), HEAD)
        if not direct:
            return pltpu.make_async_copy(outgoing.at[k], out_ref.at[rows_at, :], own_sem.at[k])
        at = pl.ds(pl.multiple_of(group * cap, cap), cap)
        return pltpu.make_async_copy(outgoing.at[k, :, at], out_ref.at[rows_at, at], own_sem.at[k])

    total_chunks = (tp - 1) * chunks
    final_at = jnp.where(
        edge, tp + 1, jnp.maximum((tp - 1 - z) * chunks + z, z * chunks + tp - 1 - z)
    )

    @pl.loop(0, total_chunks + tp + chunks)
    def _(step):
        right_turn = step - z
        right_index = (tp - 1 - right_turn // chunks) * chunks + lax.rem(right_turn, chunks)
        left_index = step - (tp - 1 - z)

        @pl.when((z > 0) & (z < tp - 1) & (right_turn >= 0) & (right_turn < (tp - 1 - z) * chunks))
        def _():
            to_right(right_index).wait_recv()
            sendbuf[right_index] = (part[right_index] + from_left[right_index].astype(F32)).astype(BF16)
            to_right(right_index).start()

        @pl.when((z > 0) & (z < tp - 1) & (left_index >= 0) & (left_index < z * chunks))
        def _():
            to_left(left_index).wait_recv()
            sendbuf[left_index] = (part[left_index] + from_right[left_index].astype(F32)).astype(BF16)
            to_left(left_index).start()

        @pl.when((z == 0) & (step >= ahead) & (step < total_chunks))
        def _():
            before_turn = step - ahead
            to_right((tp - 1 - before_turn // chunks) * chunks + lax.rem(before_turn, chunks)).wait_send()
            to_right(right_index).start()

        @pl.when((z == tp - 1) & (step >= ahead) & (step < total_chunks))
        def _():
            to_left(step - ahead).wait_send()
            to_left(step).start()

        @pl.when((step >= final_at) & (step < final_at + chunks))
        def _():
            k = step - final_at
            index = z * chunks + k

            @pl.when(z < tp - 1)
            def _():
                to_left(index).wait_recv()
                part[index] = part[index] + from_right[index].astype(F32)

            @pl.when(z > 0)
            def _():
                to_right(index).wait_recv()
                part[index] = part[index] + from_left[index].astype(F32)

            value = part[index] * scale[...]
            turned = value * cosine[...] + pltpu.roll(value, HEAD // 2, 1) * sine[...]
            rotated = jnp.where(index < key_heads, turned, value).T.astype(BF16)
            if direct:
                for r in range(1, dp + 1):
                    target = lax.rem(group + r, dp)
                    at = pl.ds(pl.multiple_of(target * cap, cap), cap)
                    outgoing[k, :, at] = jnp.dot(
                        rotated, places[:, at], preferred_element_type=F32
                    ).astype(BF16)
                    if r < dp:
                        out_copy(k, r, group, target).start()
            else:
                outgoing[k] = jnp.dot(rotated, places[...], preferred_element_type=F32).astype(BF16)
            own_copy(k).start()

    @pl.loop(0, tp * chunks)
    def _(index):
        dest = index // chunks

        @pl.when((dest > z) & ((z > 0) | ((dest == 1) & (index >= 2 * chunks - ahead))))
        def _():
            to_right(index).wait_send()

        @pl.when((dest < z) & ((z < tp - 1) | (index >= total_chunks - ahead)))
        def _():
            to_left(index).wait_send()

    for k in range(chunks):
        own_copy(k).wait()
        if direct:
            for r in range(1, dp):
                out_copy(k, r, group, lax.rem(group + r, dp)).wait_send()
                out_copy(k, r, lax.rem(group + dp - r, dp), group).wait_recv()


def per_device(hidden, norm_gain, kv_weight, owners, offsets):
    dp, tp = lax.axis_size("dp"), lax.axis_size("tp")
    rows, features = hidden.shape
    cap = 2 * rows // dp
    columns = kv_weight.shape[1]
    share = columns // tp
    chunks = share // HEAD
    direct = cap % 128 == 0
    exponent = (np.arange(HEAD) % (HEAD // 2)) * (2.0 / HEAD)
    inverse = jnp.asarray((ROPE_BASE ** (-exponent)).astype(np.float32)[None, :])
    vmem = pl.BlockSpec(memory_space=pltpu.VMEM)
    hbm = pl.BlockSpec(memory_space=pl.ANY)
    pieces = tp * chunks
    dma = pltpu.SemaphoreType.DMA
    result = pl.pallas_call(
        functools.partial(kernel, tp, dp, chunks, cap, columns // (2 * HEAD), direct),
        out_shape=jax.ShapeDtypeStruct((share, dp * cap), BF16),
        in_specs=[hbm, vmem, hbm, vmem, vmem, vmem],
        out_specs=pl.BlockSpec(memory_space=pl.ANY),
        scratch_shapes=[
            pltpu.VMEM((rows, features), BF16),
            pltpu.VMEM((features, columns), BF16),
            pltpu.VMEM((rows, features), BF16),
            pltpu.VMEM((rows, 128), F32),
            pltpu.VMEM((pieces, rows, HEAD), F32),
            pltpu.VMEM((pieces, rows, HEAD), BF16),
            pltpu.VMEM((pieces, rows, HEAD), BF16),
            pltpu.VMEM((pieces, rows, HEAD), BF16),
            pltpu.VMEM((tp, 8, rows), F32),
            pltpu.VMEM((rows, dp * cap), BF16),
            pltpu.VMEM((rows, HEAD), F32),
            pltpu.VMEM((rows, HEAD), F32),
            pltpu.VMEM((rows, HEAD), F32),
            pltpu.VMEM((chunks, HEAD, dp * cap), BF16),
            dma((tp,)), dma((tp,)), dma((pieces,)), dma((pieces,)), dma((pieces,)),
            dma((chunks, dp)), dma((chunks, dp)), dma((chunks,)),
            dma((BANDS,)), dma((tp,)),
        ],
        compiler_params=pltpu.CompilerParams(
            collective_id=0, has_side_effects=True, vmem_limit_bytes=56 * 1024 * 1024
        ),
    )(hidden, norm_gain.reshape(features // 128, 128), kv_weight, owners.reshape(1, rows), offsets.reshape(1, rows), inverse)
    if direct:
        return result
    received = lax.all_to_all(
        result.reshape(share, dp, cap), "dp", split_axis=1, concat_axis=1, tiled=True
    )
    return received.reshape(share, dp * cap)


def solution(mesh):
    in_specs = (P("dp", "tp"), P("tp"), P("tp", None), P("dp", None), P("dp"))
    out_specs = P("tp", "dp")
    return jax.shard_map(
        per_device, mesh=mesh, in_specs=in_specs, out_specs=out_specs, check_vma=False
    )
```

```python
import functools

import jax
import jax.numpy as jnp
import numpy as np
from jax import lax
from jax.experimental import pallas as pl
from jax.experimental.pallas import tpu as pltpu
from jax.sharding import PartitionSpec as P

HEAD = 128
EPSILON = 1e-05
ROPE_BASE = 500000.0
MESH = pl.DeviceIdType.MESH
SPLIT = 2
F32 = jnp.float32
BF16 = jnp.bfloat16
EXACT = lax.Precision.HIGHEST


def to_columns(rows):
    weight = jnp.full((rows.shape[0], 128), 0.125, F32)
    return lax.dot_general(
        rows, weight, (((0,), (0,)), ((), ())), precision=EXACT, preferred_element_type=F32
    )


def kernel(
    tp, dp, chunks, cap, key_heads, direct,
    h_hbm, g_ref, w_hbm, owner_ref, offset_ref, inverse_ref, out_ref,
    h_ref, w_ref, gain, scaled, squares, part, sendbuf, from_left, from_right, totals, places,
    cosine, sine, scale, outgoing,
    total_send, total_recv, send_sem, left_recv, right_recv, out_send, out_recv, own_sem, h_sem, w_sem,
):
    z = lax.axis_index("tp")
    group = lax.axis_index("dp")
    rows, features = h_ref.shape
    width = chunks * HEAD
    half = HEAD // 2 // SPLIT
    slots = dp * cap
    pieces = chunks * SPLIT
    stream = (tp - 1) * pieces
    edge = (z == 0) | (z == tp - 1)

    barrier = pltpu.get_barrier_semaphore()
    for r in range(1, tp):
        pl.semaphore_signal(barrier, inc=1, device_id={"tp": lax.rem(z + r, tp)}, device_id_type=MESH)
    if direct:
        for r in range(1, dp):
            pl.semaphore_signal(barrier, inc=1, device_id={"dp": lax.rem(group + r, dp)}, device_id_type=MESH)

    def h_copy():
        return pltpu.make_async_copy(h_hbm, h_ref, h_sem.at[0])

    def w_copy(turn):
        dest = jnp.where(z == tp - 1, turn, tp - 1 - turn)
        at = pl.ds(pl.multiple_of(dest * width, HEAD), width)
        return pltpu.make_async_copy(w_hbm.at[:, at], w_ref.at[:, at], w_sem.at[turn])

    w_copy(0).start()
    h_copy().start()
    for turn in range(1, tp):
        w_copy(turn).start()

    for i in range(features // 128):
        gain[i * 128:(i + 1) * 128, :] = to_columns(jnp.broadcast_to(g_ref[i:i + 1, :], (8, 128)))

    def to_right(index):
        return pltpu.make_async_remote_copy(
            src_ref=sendbuf.at[index], dst_ref=from_left.at[index],
            send_sem=send_sem.at[index], recv_sem=left_recv.at[index],
            device_id={"tp": jnp.minimum(z + 1, tp - 1)}, device_id_type=MESH,
        )

    def to_left(index):
        return pltpu.make_async_remote_copy(
            src_ref=sendbuf.at[index], dst_ref=from_right.at[index],
            send_sem=send_sem.at[index], recv_sem=right_recv.at[index],
            device_id={"tp": jnp.maximum(z - 1, 0)}, device_id_type=MESH,
        )

    def right_piece(n):
        return (tp - 1 - n // pieces) * pieces + lax.rem(n, pieces)

    tile = rows // 2

    def scale_weights(turn, k):
        dest = jnp.where(z == tp - 1, turn, tp - 1 - turn)
        columns = pl.ds(pl.multiple_of(dest * width + k * HEAD, HEAD), HEAD)
        scaled[...] = (w_ref[:, columns].astype(F32) * gain[...]).astype(BF16)

    def multiply(turn, k):
        dest = jnp.where(z == tp - 1, turn, tp - 1 - turn)
        for first in range(0, rows, tile):
            term = jnp.dot(h_ref[first:first + tile, :], scaled[...], preferred_element_type=F32).T
            for q in range(SPLIT):
                index = (dest * chunks + k) * SPLIT + q
                for side in range(2):
                    piece = term[side * (HEAD // 2) + q * half:side * (HEAD // 2) + (q + 1) * half, :]
                    part[index, side, :, first:first + tile] = piece
                    sendbuf[index, side, :, first:first + tile] = piece.astype(BF16)

    def start_pieces(k):
        for q in range(SPLIT):
            @pl.when(z == 0)
            def _():
                to_right((tp - 1) * pieces + k * SPLIT + q).start()

            @pl.when(z == tp - 1)
            def _():
                to_left(k * SPLIT + q).start()

    w_copy(0).wait()
    scale_weights(0, 0)
    h_copy().wait()
    multiply(0, 0)
    pl.semaphore_wait(barrier, tp - 1 + (dp - 1 if direct else 0))
    start_pieces(0)

    @pl.loop(1, chunks)
    def _(k):
        scale_weights(0, k)
        multiply(0, k)
        start_pieces(k)

    @pl.loop(1, tp)
    def _(turn):
        w_copy(turn).wait()

        @pl.loop(0, chunks)
        def _(k):
            scale_weights(turn, k)
            multiply(turn, k)

    def add_squares(step, carry):
        at = pl.ds(pl.multiple_of(step * 32, 32), 32)
        total = jnp.zeros((32, 128), F32)
        for lane in range(0, features, 128):
            wide = h_ref[at, lane:lane + 128].astype(F32)
            total = total + wide * wide
        squares[at, :] = total
        return carry

    lax.fori_loop(0, rows // 32, add_squares, 0, unroll=4)
    totals[z] = lax.dot_general(
        jnp.ones((8, 128), F32), squares[...], (((1,), (1,)), ((), ())),
        precision=EXACT, preferred_element_type=F32,
    )
    total_copies = []
    for r in range(1, tp):
        copy = pltpu.make_async_remote_copy(
            src_ref=totals.at[z], dst_ref=totals.at[z],
            send_sem=total_send.at[r], recv_sem=total_recv.at[r],
            device_id={"tp": lax.rem(z + r, tp)}, device_id_type=MESH,
        )
        copy.start()
        total_copies.append(copy)

    owner = to_columns(jnp.broadcast_to(owner_ref[...].astype(F32), (8, rows)))
    lane = lax.broadcasted_iota(jnp.int32, (1, 128), 1).astype(F32)
    named = jnp.where(owner == lane, 1.0, 0.0)
    earlier = jnp.where(
        lax.broadcasted_iota(jnp.int32, (rows, rows), 0) > lax.broadcasted_iota(jnp.int32, (rows, rows), 1),
        1.0, 0.0,
    ).astype(BF16)
    before = jnp.dot(earlier, named.astype(BF16), preferred_element_type=F32)
    rank = jnp.sum(before * named, axis=1, keepdims=True)
    slot = owner[:, 0:1] * cap + rank
    for first in range(0, slots, 256):
        here = (lax.broadcasted_iota(jnp.int32, (1, 256), 1) + first).astype(F32)
        places[:, first:first + 256] = jnp.where(slot == here, 1.0, 0.0).astype(BF16)
    offset = offset_ref[...].astype(F32)
    for q in range(SPLIT):
        angle = inverse_ref[q * half:(q + 1) * half, 0:1] * offset
        cosine[q] = jnp.cos(angle)
        sine[q] = jnp.sin(angle)

    for r in range(1, tp):
        total_copies[r - 1].wait()
    total = totals[0]
    for other in range(1, tp):
        total = total + totals[other]
    scale[...] = lax.rsqrt(total[0:1, :] / (features * tp) + EPSILON)

    def out_copy(index, r, sender, target):
        return pltpu.make_async_remote_copy(
            src_ref=outgoing.at[index, :, :, pl.ds(pl.multiple_of(target * cap, cap), cap)],
            dst_ref=out_ref.at[index // SPLIT, :, lax.rem(index, SPLIT), :, pl.ds(pl.multiple_of(sender * cap, cap), cap)],
            send_sem=out_send.at[index, r], recv_sem=out_recv.at[index, r],
            device_id={"dp": target}, device_id_type=MESH,
        )

    def own_copy(index):
        home = out_ref.at[index // SPLIT, :, lax.rem(index, SPLIT)]
        if not direct:
            return pltpu.make_async_copy(outgoing.at[index], home, own_sem.at[index])
        at = pl.ds(pl.multiple_of(group * cap, cap), cap)
        return pltpu.make_async_copy(
            outgoing.at[index, :, :, at],
            out_ref.at[index // SPLIT, :, lax.rem(index, SPLIT), :, at], own_sem.at[index],
        )

    final_at = jnp.where(
        edge, stream // 2 + 1, jnp.maximum((tp - 1 - z) * pieces + z, z * pieces + tp - 1 - z)
    )

    @pl.loop(0, stream + tp + pieces)
    def _(step):
        right_turn = step - z
        right_index = right_piece(right_turn)
        left_index = step - (tp - 1 - z)

        @pl.when((z > 0) & (z < tp - 1) & (right_turn >= 0) & (right_turn < (tp - 1 - z) * pieces))
        def _():
            to_right(right_index).wait_recv()
            sendbuf[right_index] = (part[right_index] + from_left[right_index].astype(F32)).astype(BF16)
            to_right(right_index).start()

        @pl.when((z > 0) & (z < tp - 1) & (left_index >= 0) & (left_index < z * pieces))
        def _():
            to_left(left_index).wait_recv()
            sendbuf[left_index] = (part[left_index] + from_right[left_index].astype(F32)).astype(BF16)
            to_left(left_index).start()

        @pl.when((z == 0) & (step >= 2) & (step < stream))
        def _():
            to_right(right_piece(step - 2)).wait_send()

            @pl.when(step >= pieces)
            def _():
                to_right(right_index).start()

        @pl.when((z == tp - 1) & (step >= 2) & (step < stream))
        def _():
            to_left(step - 2).wait_send()

            @pl.when(step >= pieces)
            def _():
                to_left(step).start()

        @pl.when((step >= final_at) & (step < final_at + pieces))
        def _():
            place = step - final_at
            index = z * pieces + place
            q = lax.rem(place, SPLIT)

            @pl.when(z < tp - 1)
            def _():
                to_left(index).wait_recv()
                part[index] = part[index] + from_right[index].astype(F32)

            @pl.when(z > 0)
            def _():
                to_right(index).wait_recv()
                part[index] = part[index] + from_left[index].astype(F32)

            first = part[index, 0] * scale[...]
            second = part[index, 1] * scale[...]
            is_key = index // SPLIT < key_heads
            cos, sin = cosine[q], sine[q]
            turned = jnp.concatenate(
                [
                    jnp.where(is_key, first * cos - second * sin, first).astype(BF16),
                    jnp.where(is_key, second * cos + first * sin, second).astype(BF16),
                ],
                axis=0,
            )
            if direct:
                for r in range(1, dp + 1):
                    target = lax.rem(group + r, dp)
                    at = pl.ds(pl.multiple_of(target * cap, cap), cap)
                    outgoing[place, :, :, at] = jnp.dot(
                        turned, places[:, at], preferred_element_type=F32
                    ).astype(BF16).reshape(2, half, cap)
                    if r < dp:
                        out_copy(place, r, group, target).start()
            else:
                outgoing[place] = jnp.dot(
                    turned, places[...], preferred_element_type=F32
                ).astype(BF16).reshape(2, half, slots)
            own_copy(place).start()

    @pl.loop(0, tp * pieces)
    def _(index):
        dest = index // pieces

        @pl.when((dest > z) & ((z > 0) | ((dest == 1) & (index >= 2 * pieces - 2))))
        def _():
            to_right(index).wait_send()

        @pl.when((dest < z) & ((z < tp - 1) | (index >= stream - 2)))
        def _():
            to_left(index).wait_send()

    @pl.loop(0, pieces)
    def _(place):
        own_copy(place).wait()
        if direct:
            for r in range(1, dp):
                out_copy(place, r, group, lax.rem(group + r, dp)).wait_send()
                out_copy(place, r, lax.rem(group + dp - r, dp), group).wait_recv()


def per_device(hidden, norm_gain, kv_weight, owners, offsets):
    dp, tp = lax.axis_size("dp"), lax.axis_size("tp")
    rows, features = hidden.shape
    cap = 2 * rows // dp
    columns = kv_weight.shape[1]
    share = columns // tp
    chunks = share // HEAD
    direct = cap % 128 == 0
    exponent = np.arange(HEAD // 2) * (2.0 / HEAD)
    inverse = np.repeat((ROPE_BASE ** (-exponent)).astype(np.float32)[:, None], 128, axis=1)
    vmem = pl.BlockSpec(memory_space=pltpu.VMEM)
    hbm = pl.BlockSpec(memory_space=pl.ANY)
    pieces = chunks * SPLIT
    half = HEAD // 2 // SPLIT
    dma = pltpu.SemaphoreType.DMA
    result = pl.pallas_call(
        functools.partial(kernel, tp, dp, chunks, cap, columns // (2 * HEAD), direct),
        out_shape=jax.ShapeDtypeStruct((chunks, 2, SPLIT, half, dp * cap), BF16),
        in_specs=[hbm, vmem, hbm, vmem, vmem, vmem],
        out_specs=hbm,
        scratch_shapes=[
            pltpu.VMEM((rows, features), BF16),
            pltpu.VMEM((features, columns), BF16),
            pltpu.VMEM((features, 128), F32),
            pltpu.VMEM((features, HEAD), BF16),
            pltpu.VMEM((rows, 128), F32),
            pltpu.VMEM((tp * pieces, 2, half, rows), F32),
            pltpu.VMEM((tp * pieces, 2, half, rows), BF16),
            pltpu.VMEM((tp * pieces, 2, half, rows), BF16),
            pltpu.VMEM((tp * pieces, 2, half, rows), BF16),
            pltpu.VMEM((tp, 8, rows), F32),
            pltpu.VMEM((rows, dp * cap), BF16),
            pltpu.VMEM((SPLIT, half, rows), F32),
            pltpu.VMEM((SPLIT, half, rows), F32),
            pltpu.VMEM((1, rows), F32),
            pltpu.VMEM((pieces, 2, half, dp * cap), BF16),
            dma((tp,)), dma((tp,)), dma((tp * pieces,)), dma((tp * pieces,)), dma((tp * pieces,)),
            dma((pieces, dp)), dma((pieces, dp)), dma((pieces,)), dma((1,)), dma((tp,)),
        ],
        compiler_params=pltpu.CompilerParams(
            collective_id=0, has_side_effects=True, vmem_limit_bytes=56 * 1024 * 1024
        ),
    )(hidden, norm_gain.reshape(features // 128, 128), kv_weight, owners.reshape(1, rows), offsets.reshape(1, rows), jnp.asarray(inverse))
    result = result.reshape(share, dp * cap)
    if direct:
        return result
    received = lax.all_to_all(
        result.reshape(share, dp, cap), "dp", split_axis=1, concat_axis=1, tiled=True
    )
    return received.reshape(share, dp * cap)


def solution(mesh):
    in_specs = (P("dp", "tp"), P("tp"), P("tp", None), P("dp", None), P("dp"))
    out_specs = P("tp", "dp")
    return jax.shard_map(
        per_device, mesh=mesh, in_specs=in_specs, out_specs=out_specs, check_vma=False
    )
```

```python
import functools

import jax
import jax.numpy as jnp
import numpy as np
from jax import lax
from jax.experimental import pallas as pl
from jax.experimental.pallas import tpu as pltpu
from jax.sharding import PartitionSpec as P

HEAD = 128
EPSILON = 1e-05
ROPE_BASE = 500000.0
MESH = pl.DeviceIdType.MESH
SPLIT = 2
F32 = jnp.float32
BF16 = jnp.bfloat16
EXACT = lax.Precision.HIGHEST


def to_columns(rows):
    weight = jnp.full((rows.shape[0], 128), 0.125, F32)
    return lax.dot_general(
        rows, weight, (((0,), (0,)), ((), ())), precision=EXACT, preferred_element_type=F32
    )


def kernel(
    tp, dp, chunks, cap, key_heads, direct,
    h_hbm, g_ref, w_hbm, owner_ref, offset_ref, inverse_ref, out_ref,
    h_ref, w_ref, gain, scaled, squares, part, sendbuf, from_left, from_right, totals, places,
    cosine, sine, scale, outgoing,
    total_send, total_recv, send_sem, left_recv, right_recv, out_send, out_recv, own_sem, h_sem, w_sem,
):
    z = lax.axis_index("tp")
    group = lax.axis_index("dp")
    rows, features = h_ref.shape
    width = chunks * HEAD
    half = HEAD // 2 // SPLIT
    slots = dp * cap
    pieces = chunks * SPLIT
    stream = (tp - 1) * pieces
    edge = (z == 0) | (z == tp - 1)

    barrier = pltpu.get_barrier_semaphore()
    for r in range(1, tp):
        pl.semaphore_signal(barrier, inc=1, device_id={"tp": lax.rem(z + r, tp)}, device_id_type=MESH)
    if direct:
        for r in range(1, dp):
            pl.semaphore_signal(barrier, inc=1, device_id={"dp": lax.rem(group + r, dp)}, device_id_type=MESH)

    def h_copy():
        return pltpu.make_async_copy(h_hbm, h_ref, h_sem.at[0])

    def w_copy(turn):
        dest = jnp.where(z == tp - 1, turn, tp - 1 - turn)
        at = pl.ds(pl.multiple_of(dest * width, HEAD), width)
        return pltpu.make_async_copy(w_hbm.at[:, at], w_ref.at[:, at], w_sem.at[turn])

    w_copy(0).start()
    h_copy().start()
    for turn in range(1, tp):
        w_copy(turn).start()

    for i in range(features // 128):
        gain[i * 128:(i + 1) * 128, :] = to_columns(jnp.broadcast_to(g_ref[i:i + 1, :], (8, 128)))

    def to_right(index):
        return pltpu.make_async_remote_copy(
            src_ref=sendbuf.at[index], dst_ref=from_left.at[index],
            send_sem=send_sem.at[index], recv_sem=left_recv.at[index],
            device_id={"tp": jnp.minimum(z + 1, tp - 1)}, device_id_type=MESH,
        )

    def to_left(index):
        return pltpu.make_async_remote_copy(
            src_ref=sendbuf.at[index], dst_ref=from_right.at[index],
            send_sem=send_sem.at[index], recv_sem=right_recv.at[index],
            device_id={"tp": jnp.maximum(z - 1, 0)}, device_id_type=MESH,
        )

    hops = tp - 1

    def right_piece(n):
        return (hops - lax.rem(n, hops)) * pieces + n // hops

    def left_piece(n):
        return lax.rem(n, hops) * pieces + n // hops

    tile = rows // 2

    def scale_weights(turn, k):
        dest = jnp.where(z == tp - 1, turn, tp - 1 - turn)
        columns = pl.ds(pl.multiple_of(dest * width + k * HEAD, HEAD), HEAD)
        scaled[...] = (w_ref[:, columns].astype(F32) * gain[...]).astype(BF16)

    def multiply(turn, k):
        dest = jnp.where(z == tp - 1, turn, tp - 1 - turn)
        for first in range(0, rows, tile):
            term = jnp.dot(h_ref[first:first + tile, :], scaled[...], preferred_element_type=F32).T
            for q in range(SPLIT):
                index = (dest * chunks + k) * SPLIT + q
                for side in range(2):
                    piece = term[side * (HEAD // 2) + q * half:side * (HEAD // 2) + (q + 1) * half, :]
                    part[index, side, :, first:first + tile] = piece
                    sendbuf[index, side, :, first:first + tile] = piece.astype(BF16)

    def start_pieces(turn, k):
        for q in range(SPLIT):
            n = (k * SPLIT + q) * hops + turn

            @pl.when(z == 0)
            def _():
                to_right(right_piece(n)).start()

            @pl.when(z == tp - 1)
            def _():
                to_left(left_piece(n)).start()

    def head_products(k, send):
        @pl.loop(0, tp)
        def _(turn):
            scale_weights(turn, k)
            multiply(turn, k)
            if send:
                @pl.when(turn < hops)
                def _():
                    start_pieces(turn, k)

    w_copy(0).wait()
    scale_weights(0, 0)
    h_copy().wait()
    multiply(0, 0)
    pl.semaphore_wait(barrier, tp - 1 + (dp - 1 if direct else 0))
    start_pieces(0, 0)

    @pl.loop(1, tp)
    def _(turn):
        w_copy(turn).wait()
        scale_weights(turn, 0)
        multiply(turn, 0)

        @pl.when(turn < hops)
        def _():
            start_pieces(turn, 0)

    def add_squares(step, carry):
        at = pl.ds(pl.multiple_of(step * 32, 32), 32)
        total = jnp.zeros((32, 128), F32)
        for lane in range(0, features, 128):
            wide = h_ref[at, lane:lane + 128].astype(F32)
            total = total + wide * wide
        squares[at, :] = total
        return carry

    lax.fori_loop(0, rows // 32, add_squares, 0, unroll=4)
    totals[z] = lax.dot_general(
        jnp.ones((8, 128), F32), squares[...], (((1,), (1,)), ((), ())),
        precision=EXACT, preferred_element_type=F32,
    )
    total_copies = []
    for r in range(1, tp):
        copy = pltpu.make_async_remote_copy(
            src_ref=totals.at[z], dst_ref=totals.at[z],
            send_sem=total_send.at[r], recv_sem=total_recv.at[r],
            device_id={"tp": lax.rem(z + r, tp)}, device_id_type=MESH,
        )
        copy.start()
        total_copies.append(copy)

    owner = to_columns(jnp.broadcast_to(owner_ref[...].astype(F32), (8, rows)))
    lane = lax.broadcasted_iota(jnp.int32, (1, 128), 1).astype(F32)
    named = jnp.where(owner == lane, 1.0, 0.0)
    earlier = jnp.where(
        lax.broadcasted_iota(jnp.int32, (rows, rows), 0) > lax.broadcasted_iota(jnp.int32, (rows, rows), 1),
        1.0, 0.0,
    ).astype(BF16)
    before = jnp.dot(earlier, named.astype(BF16), preferred_element_type=F32)
    rank = jnp.sum(before * named, axis=1, keepdims=True)
    slot = owner[:, 0:1] * cap + rank
    for first in range(0, slots, 256):
        here = (lax.broadcasted_iota(jnp.int32, (1, 256), 1) + first).astype(F32)
        places[:, first:first + 256] = jnp.where(slot == here, 1.0, 0.0).astype(BF16)
    offset = offset_ref[...].astype(F32)
    for q in range(SPLIT):
        angle = inverse_ref[q * half:(q + 1) * half, 0:1] * offset
        cosine[q] = jnp.cos(angle)
        sine[q] = jnp.sin(angle)

    for r in range(1, tp):
        total_copies[r - 1].wait()
    total = totals[0]
    for other in range(1, tp):
        total = total + totals[other]
    scale[...] = lax.rsqrt(total[0:1, :] / (features * tp) + EPSILON)

    def out_copy(index, r, sender, target):
        return pltpu.make_async_remote_copy(
            src_ref=outgoing.at[index, :, :, pl.ds(pl.multiple_of(target * cap, cap), cap)],
            dst_ref=out_ref.at[index // SPLIT, :, lax.rem(index, SPLIT), :, pl.ds(pl.multiple_of(sender * cap, cap), cap)],
            send_sem=out_send.at[index, r], recv_sem=out_recv.at[index, r],
            device_id={"dp": target}, device_id_type=MESH,
        )

    def own_copy(index):
        home = out_ref.at[index // SPLIT, :, lax.rem(index, SPLIT)]
        if not direct:
            return pltpu.make_async_copy(outgoing.at[index], home, own_sem.at[index])
        at = pl.ds(pl.multiple_of(group * cap, cap), cap)
        return pltpu.make_async_copy(
            outgoing.at[index, :, :, at],
            out_ref.at[index // SPLIT, :, lax.rem(index, SPLIT), :, at], own_sem.at[index],
        )

    ahead = min(chunks, 2) * SPLIT * hops

    @pl.loop(0, stream + tp)
    def _(step):
        for k in range(1, chunks):
            @pl.when(step == jnp.where(edge, 0, (k - 1) * SPLIT * hops + 2))
            def _():
                head_products(k, k == 1)

        from_z0 = step - z
        from_end = step - (tp - 1 - z)
        right_dest = hops - lax.rem(jnp.maximum(from_z0, 0), hops)
        left_dest = lax.rem(jnp.maximum(from_end, 0), hops)

        @pl.when((z > 0) & (from_z0 >= 0) & (from_z0 < stream) & (right_dest > z))
        def _():
            index = right_piece(from_z0)
            to_right(index).wait_recv()
            sendbuf[index] = (part[index] + from_left[index].astype(F32)).astype(BF16)
            to_right(index).start()

        @pl.when((z < tp - 1) & (from_end >= 0) & (from_end < stream) & (left_dest < z))
        def _():
            index = left_piece(from_end)
            to_left(index).wait_recv()
            sendbuf[index] = (part[index] + from_right[index].astype(F32)).astype(BF16)
            to_left(index).start()

        @pl.when((z == 0) & (step >= 2) & (step < stream))
        def _():
            to_right(right_piece(step - 2)).wait_send()

            @pl.when(step >= ahead)
            def _():
                to_right(right_piece(step)).start()

        @pl.when((z == tp - 1) & (step >= 2) & (step < stream))
        def _():
            to_left(left_piece(step - 2)).wait_send()

            @pl.when(step >= ahead)
            def _():
                to_left(left_piece(step)).start()

        def finish(place):
            index = z * pieces + place
            q = lax.rem(place, SPLIT)

            @pl.when(z < tp - 1)
            def _():
                to_left(index).wait_recv()
                part[index] = part[index] + from_right[index].astype(F32)

            @pl.when(z > 0)
            def _():
                to_right(index).wait_recv()
                part[index] = part[index] + from_left[index].astype(F32)

            first = part[index, 0] * scale[...]
            second = part[index, 1] * scale[...]
            is_key = index // SPLIT < key_heads
            cos, sin = cosine[q], sine[q]
            turned = jnp.concatenate(
                [
                    jnp.where(is_key, first * cos - second * sin, first).astype(BF16),
                    jnp.where(is_key, second * cos + first * sin, second).astype(BF16),
                ],
                axis=0,
            )
            if direct:
                for r in range(1, dp + 1):
                    target = lax.rem(group + r, dp)
                    at = pl.ds(pl.multiple_of(target * cap, cap), cap)
                    outgoing[place, :, :, at] = jnp.dot(
                        turned, places[:, at], preferred_element_type=F32
                    ).astype(BF16).reshape(2, half, cap)
                    if r < dp:
                        out_copy(place, r, group, target).start()
            else:
                outgoing[place] = jnp.dot(
                    turned, places[...], preferred_element_type=F32
                ).astype(BF16).reshape(2, half, slots)
            own_copy(place).start()

        late = stream // 2 + 1
        catch = jnp.clip(step - late, 0, pieces)
        on_time = (step - 1) // hops - 1
        at_end = (step >= late) & (step < late + pieces) & ((catch + 1) * hops + 1 <= step)
        at_end_late = (step >= 1) & (lax.rem(step + hops - 1, hops) == 0) & (late + on_time < step)
        place = jnp.where(edge, jnp.where(at_end, catch, on_time), step // hops - 1)
        due = jnp.where(edge, at_end | at_end_late, lax.rem(step, hops) == 0)

        @pl.when(due & (place >= 0) & (place < pieces))
        def _():
            finish(place)

    @pl.loop(0, stream)
    def _(n):
        @pl.when((hops - lax.rem(n, hops) > z) & ((z > 0) | (n >= stream - 2)))
        def _():
            to_right(right_piece(n)).wait_send()

        @pl.when((lax.rem(n, hops) < z) & ((z < tp - 1) | (n >= stream - 2)))
        def _():
            to_left(left_piece(n)).wait_send()

    @pl.loop(0, pieces)
    def _(place):
        own_copy(place).wait()
        if direct:
            for r in range(1, dp):
                out_copy(place, r, group, lax.rem(group + r, dp)).wait_send()
                out_copy(place, r, lax.rem(group + dp - r, dp), group).wait_recv()


def per_device(hidden, norm_gain, kv_weight, owners, offsets):
    dp, tp = lax.axis_size("dp"), lax.axis_size("tp")
    rows, features = hidden.shape
    cap = 2 * rows // dp
    columns = kv_weight.shape[1]
    share = columns // tp
    chunks = share // HEAD
    direct = cap % 128 == 0
    exponent = np.arange(HEAD // 2) * (2.0 / HEAD)
    inverse = np.repeat((ROPE_BASE ** (-exponent)).astype(np.float32)[:, None], 128, axis=1)
    vmem = pl.BlockSpec(memory_space=pltpu.VMEM)
    hbm = pl.BlockSpec(memory_space=pl.ANY)
    pieces = chunks * SPLIT
    half = HEAD // 2 // SPLIT
    dma = pltpu.SemaphoreType.DMA
    result = pl.pallas_call(
        functools.partial(kernel, tp, dp, chunks, cap, columns // (2 * HEAD), direct),
        out_shape=jax.ShapeDtypeStruct((chunks, 2, SPLIT, half, dp * cap), BF16),
        in_specs=[hbm, vmem, hbm, vmem, vmem, vmem],
        out_specs=hbm,
        scratch_shapes=[
            pltpu.VMEM((rows, features), BF16),
            pltpu.VMEM((features, columns), BF16),
            pltpu.VMEM((features, 128), F32),
            pltpu.VMEM((features, HEAD), BF16),
            pltpu.VMEM((rows, 128), F32),
            pltpu.VMEM((tp * pieces, 2, half, rows), F32),
            pltpu.VMEM((tp * pieces, 2, half, rows), BF16),
            pltpu.VMEM((tp * pieces, 2, half, rows), BF16),
            pltpu.VMEM((tp * pieces, 2, half, rows), BF16),
            pltpu.VMEM((tp, 8, rows), F32),
            pltpu.VMEM((rows, dp * cap), BF16),
            pltpu.VMEM((SPLIT, half, rows), F32),
            pltpu.VMEM((SPLIT, half, rows), F32),
            pltpu.VMEM((1, rows), F32),
            pltpu.VMEM((pieces, 2, half, dp * cap), BF16),
            dma((tp,)), dma((tp,)), dma((tp * pieces,)), dma((tp * pieces,)), dma((tp * pieces,)),
            dma((pieces, dp)), dma((pieces, dp)), dma((pieces,)), dma((1,)), dma((tp,)),
        ],
        compiler_params=pltpu.CompilerParams(
            collective_id=0, has_side_effects=True, vmem_limit_bytes=56 * 1024 * 1024
        ),
    )(hidden, norm_gain.reshape(features // 128, 128), kv_weight, owners.reshape(1, rows), offsets.reshape(1, rows), jnp.asarray(inverse))
    result = result.reshape(share, dp * cap)
    if direct:
        return result
    received = lax.all_to_all(
        result.reshape(share, dp, cap), "dp", split_axis=1, concat_axis=1, tiled=True
    )
    return received.reshape(share, dp * cap)


def solution(mesh):
    in_specs = (P("dp", "tp"), P("tp"), P("tp", None), P("dp", None), P("dp"))
    out_specs = P("tp", "dp")
    return jax.shard_map(
        per_device, mesh=mesh, in_specs=in_specs, out_specs=out_specs, check_vma=False
    )
```

```python
import functools

import jax
import jax.numpy as jnp
import numpy as np
from jax import lax
from jax.experimental import pallas as pl
from jax.experimental.pallas import tpu as pltpu
from jax.sharding import PartitionSpec as P

HEAD = 128
EPSILON = 1e-05
ROPE_BASE = 500000.0
MESH = pl.DeviceIdType.MESH
SPLIT = 2
LAG = 2
F32 = jnp.float32
BF16 = jnp.bfloat16
EXACT = lax.Precision.HIGHEST


def to_columns(rows):
    weight = jnp.full((rows.shape[0], 128), 0.125, F32)
    return lax.dot_general(
        rows, weight, (((0,), (0,)), ((), ())), precision=EXACT, preferred_element_type=F32
    )


def kernel(
    tp, dp, chunks, cap, key_heads, direct,
    h_hbm, g_ref, w_hbm, owner_ref, offset_ref, inverse_ref, out_ref,
    h_ref, w_ref, gain, scaled, squares, part, sendbuf, from_left, from_right, totals, places,
    cosine, sine, scale, outgoing,
    total_send, total_recv, send_sem, left_recv, right_recv, out_send, out_recv, own_sem, h_sem, w_sem,
):
    z = lax.axis_index("tp")
    group = lax.axis_index("dp")
    rows, features = h_ref.shape
    width = chunks * HEAD
    half = HEAD // 2 // SPLIT
    slots = dp * cap
    pieces = chunks * SPLIT
    edge = (z == 0) | (z == tp - 1)

    barrier = pltpu.get_barrier_semaphore()
    for r in range(1, tp):
        pl.semaphore_signal(barrier, inc=1, device_id={"tp": lax.rem(z + r, tp)}, device_id_type=MESH)
    if direct:
        for r in range(1, dp):
            pl.semaphore_signal(barrier, inc=1, device_id={"dp": lax.rem(group + r, dp)}, device_id_type=MESH)

    def h_copy():
        return pltpu.make_async_copy(h_hbm, h_ref, h_sem.at[0])

    def w_copy(turn):
        dest = jnp.where(z == tp - 1, turn, tp - 1 - turn)
        at = pl.ds(pl.multiple_of(dest * width, HEAD), width)
        return pltpu.make_async_copy(w_hbm.at[:, at], w_ref.at[:, at], w_sem.at[turn])

    w_copy(0).start()
    h_copy().start()
    for turn in range(1, tp):
        w_copy(turn).start()

    for i in range(features // 128):
        gain[i * 128:(i + 1) * 128, :] = to_columns(jnp.broadcast_to(g_ref[i:i + 1, :], (8, 128)))

    def to_right(index):
        return pltpu.make_async_remote_copy(
            src_ref=sendbuf.at[index], dst_ref=from_left.at[index],
            send_sem=send_sem.at[index], recv_sem=left_recv.at[index],
            device_id={"tp": jnp.minimum(z + 1, tp - 1)}, device_id_type=MESH,
        )

    def to_left(index):
        return pltpu.make_async_remote_copy(
            src_ref=sendbuf.at[index], dst_ref=from_right.at[index],
            send_sem=send_sem.at[index], recv_sem=right_recv.at[index],
            device_id={"tp": jnp.maximum(z - 1, 0)}, device_id_type=MESH,
        )

    hops = tp - 1
    span = (pieces + hops - 1) * hops

    def piece_of(n):
        return n // hops - lax.rem(n, hops)

    def in_stream(n):
        return (n >= 0) & (n < span) & (piece_of(n) >= 0) & (piece_of(n) < pieces)

    tile = rows // 2

    def scale_weights(turn, k):
        dest = jnp.where(z == tp - 1, turn, tp - 1 - turn)
        columns = pl.ds(pl.multiple_of(dest * width + k * HEAD, HEAD), HEAD)
        scaled[...] = (w_ref[:, columns].astype(F32) * gain[...]).astype(BF16)

    def multiply(turn, k):
        dest = jnp.where(z == tp - 1, turn, tp - 1 - turn)
        for first in range(0, rows, tile):
            term = jnp.dot(h_ref[first:first + tile, :], scaled[...], preferred_element_type=F32).T
            for q in range(SPLIT):
                index = (dest * chunks + k) * SPLIT + q
                for side in range(2):
                    piece = term[side * (HEAD // 2) + q * half:side * (HEAD // 2) + (q + 1) * half, :]
                    part[index, side, :, first:first + tile] = piece
                    sendbuf[index, side, :, first:first + tile] = piece.astype(BF16)

    def start_pieces(turn, k):
        for q in range(SPLIT):
            @pl.when(z == 0)
            def _():
                to_right((hops - turn) * pieces + k * SPLIT + q).start()

            @pl.when(z == tp - 1)
            def _():
                to_left(turn * pieces + k * SPLIT + q).start()

    def head_products(k, send):
        @pl.loop(0, tp)
        def _(turn):
            scale_weights(turn, k)
            multiply(turn, k)
            if send:
                @pl.when(turn < hops)
                def _():
                    start_pieces(turn, k)

    w_copy(0).wait()
    scale_weights(0, 0)
    h_copy().wait()
    multiply(0, 0)
    pl.semaphore_wait(barrier, tp - 1 + (dp - 1 if direct else 0))
    start_pieces(0, 0)

    @pl.loop(1, tp)
    def _(turn):
        w_copy(turn).wait()
        scale_weights(turn, 0)
        multiply(turn, 0)

        @pl.when(turn < hops)
        def _():
            start_pieces(turn, 0)

    def add_squares(step, carry):
        at = pl.ds(pl.multiple_of(step * 32, 32), 32)
        total = jnp.zeros((32, 128), F32)
        for lane in range(0, features, 128):
            wide = h_ref[at, lane:lane + 128].astype(F32)
            total = total + wide * wide
        squares[at, :] = total
        return carry

    lax.fori_loop(0, rows // 32, add_squares, 0, unroll=4)
    totals[z] = lax.dot_general(
        jnp.ones((8, 128), F32), squares[...], (((1,), (1,)), ((), ())),
        precision=EXACT, preferred_element_type=F32,
    )
    total_copies = []
    for r in range(1, tp):
        copy = pltpu.make_async_remote_copy(
            src_ref=totals.at[z], dst_ref=totals.at[z],
            send_sem=total_send.at[r], recv_sem=total_recv.at[r],
            device_id={"tp": lax.rem(z + r, tp)}, device_id_type=MESH,
        )
        copy.start()
        total_copies.append(copy)

    owner = to_columns(jnp.broadcast_to(owner_ref[...].astype(F32), (8, rows)))
    lane = lax.broadcasted_iota(jnp.int32, (1, 128), 1).astype(F32)
    named = jnp.where(owner == lane, 1.0, 0.0)
    earlier = jnp.where(
        lax.broadcasted_iota(jnp.int32, (rows, rows), 0) > lax.broadcasted_iota(jnp.int32, (rows, rows), 1),
        1.0, 0.0,
    ).astype(BF16)
    before = jnp.dot(earlier, named.astype(BF16), preferred_element_type=F32)
    rank = jnp.sum(before * named, axis=1, keepdims=True)
    slot = owner[:, 0:1] * cap + rank
    for first in range(0, slots, 256):
        here = (lax.broadcasted_iota(jnp.int32, (1, 256), 1) + first).astype(F32)
        places[:, first:first + 256] = jnp.where(slot == here, 1.0, 0.0).astype(BF16)
    offset = offset_ref[...].astype(F32)
    for q in range(SPLIT):
        angle = inverse_ref[q * half:(q + 1) * half, 0:1] * offset
        cosine[q] = jnp.cos(angle)
        sine[q] = jnp.sin(angle)

    for r in range(1, tp):
        total_copies[r - 1].wait()
    total = totals[0]
    for other in range(1, tp):
        total = total + totals[other]
    scale[...] = lax.rsqrt(total[0:1, :] / (features * tp) + EPSILON)

    def out_copy(index, r, sender, target):
        return pltpu.make_async_remote_copy(
            src_ref=outgoing.at[index, :, :, pl.ds(pl.multiple_of(target * cap, cap), cap)],
            dst_ref=out_ref.at[index // SPLIT, :, lax.rem(index, SPLIT), :, pl.ds(pl.multiple_of(sender * cap, cap), cap)],
            send_sem=out_send.at[index, r], recv_sem=out_recv.at[index, r],
            device_id={"dp": target}, device_id_type=MESH,
        )

    def own_copy(index):
        home = out_ref.at[index // SPLIT, :, lax.rem(index, SPLIT)]
        if not direct:
            return pltpu.make_async_copy(outgoing.at[index], home, own_sem.at[index])
        at = pl.ds(pl.multiple_of(group * cap, cap), cap)
        return pltpu.make_async_copy(
            outgoing.at[index, :, :, at],
            out_ref.at[index // SPLIT, :, lax.rem(index, SPLIT), :, at], own_sem.at[index],
        )

    ahead = min(chunks, 2) * SPLIT
    final_at = jnp.where(
        edge, LAG * hops + hops,
        jnp.maximum((hops - z) * (hops + 1) + LAG * z, z * (hops + 1) + LAG * (hops - z)),
    )
    latest = max(
        [LAG * hops + hops] + [(hops - at) * (hops + 1) + LAG * at for at in range(1, hops)]
        + [at * (hops + 1) + LAG * (hops - at) for at in range(1, hops)]
    )

    @pl.loop(0, max(latest + (pieces - 1) * hops + 1, span + LAG * hops))
    def _(step):
        for k in range(1, chunks):
            @pl.when(step == jnp.where(edge, 0, k * SPLIT * hops - hops))
            def _():
                head_products(k, k == 1)

        from_left_slot = step - LAG * z
        from_right_slot = step - LAG * (hops - z)
        right_dest = hops - lax.rem(jnp.maximum(from_left_slot, 0), hops)
        left_dest = lax.rem(jnp.maximum(from_right_slot, 0), hops)

        @pl.when((z > 0) & in_stream(from_left_slot) & (right_dest > z))
        def _():
            index = right_dest * pieces + piece_of(from_left_slot)
            to_right(index).wait_recv()
            sendbuf[index] = (part[index] + from_left[index].astype(F32)).astype(BF16)
            to_right(index).start()

        @pl.when((z < hops) & in_stream(from_right_slot) & (left_dest < z))
        def _():
            index = left_dest * pieces + piece_of(from_right_slot)
            to_left(index).wait_recv()
            sendbuf[index] = (part[index] + from_right[index].astype(F32)).astype(BF16)
            to_left(index).start()

        @pl.when((z == 0) & in_stream(step))
        def _():
            index = right_dest * pieces + piece_of(step)

            @pl.when(piece_of(step) > 0)
            def _():
                to_right(index - 1).wait_send()

            @pl.when(piece_of(step) >= ahead)
            def _():
                to_right(index).start()

        @pl.when((z == hops) & in_stream(step))
        def _():
            index = left_dest * pieces + piece_of(step)

            @pl.when(piece_of(step) > 0)
            def _():
                to_left(index - 1).wait_send()

            @pl.when(piece_of(step) >= ahead)
            def _():
                to_left(index).start()

        def finish(place):
            index = z * pieces + place
            q = lax.rem(place, SPLIT)

            @pl.when(z < tp - 1)
            def _():
                to_left(index).wait_recv()
                part[index] = part[index] + from_right[index].astype(F32)

            @pl.when(z > 0)
            def _():
                to_right(index).wait_recv()
                part[index] = part[index] + from_left[index].astype(F32)

            first = part[index, 0] * scale[...]
            second = part[index, 1] * scale[...]
            is_key = index // SPLIT < key_heads
            cos, sin = cosine[q], sine[q]
            turned = jnp.concatenate(
                [
                    jnp.where(is_key, first * cos - second * sin, first).astype(BF16),
                    jnp.where(is_key, second * cos + first * sin, second).astype(BF16),
                ],
                axis=0,
            )
            if direct:
                for r in range(1, dp + 1):
                    target = lax.rem(group + r, dp)
                    at = pl.ds(pl.multiple_of(target * cap, cap), cap)
                    outgoing[place, :, :, at] = jnp.dot(
                        turned, places[:, at], preferred_element_type=F32
                    ).astype(BF16).reshape(2, half, cap)
                    if r < dp:
                        out_copy(place, r, group, target).start()
            else:
                outgoing[place] = jnp.dot(
                    turned, places[...], preferred_element_type=F32
                ).astype(BF16).reshape(2, half, slots)
            own_copy(place).start()

        since = step - final_at

        @pl.when((since >= 0) & (since < pieces * hops) & (lax.rem(jnp.maximum(since, 0), hops) == 0))
        def _():
            finish(jnp.maximum(since, 0) // hops)

    @pl.loop(0, tp * pieces)
    def _(index):
        dest = index // pieces
        last = lax.rem(index, pieces) == pieces - 1

        @pl.when((dest > z) & ((z > 0) | last))
        def _():
            to_right(index).wait_send()

        @pl.when((dest < z) & ((z < hops) | last))
        def _():
            to_left(index).wait_send()

    @pl.loop(0, pieces)
    def _(place):
        own_copy(place).wait()
        if direct:
            for r in range(1, dp):
                out_copy(place, r, group, lax.rem(group + r, dp)).wait_send()
                out_copy(place, r, lax.rem(group + dp - r, dp), group).wait_recv()


def per_device(hidden, norm_gain, kv_weight, owners, offsets):
    dp, tp = lax.axis_size("dp"), lax.axis_size("tp")
    rows, features = hidden.shape
    cap = 2 * rows // dp
    columns = kv_weight.shape[1]
    share = columns // tp
    chunks = share // HEAD
    direct = cap % 128 == 0
    exponent = np.arange(HEAD // 2) * (2.0 / HEAD)
    inverse = np.repeat((ROPE_BASE ** (-exponent)).astype(np.float32)[:, None], 128, axis=1)
    vmem = pl.BlockSpec(memory_space=pltpu.VMEM)
    hbm = pl.BlockSpec(memory_space=pl.ANY)
    pieces = chunks * SPLIT
    half = HEAD // 2 // SPLIT
    dma = pltpu.SemaphoreType.DMA
    result = pl.pallas_call(
        functools.partial(kernel, tp, dp, chunks, cap, columns // (2 * HEAD), direct),
        out_shape=jax.ShapeDtypeStruct((chunks, 2, SPLIT, half, dp * cap), BF16),
        in_specs=[hbm, vmem, hbm, vmem, vmem, vmem],
        out_specs=hbm,
        scratch_shapes=[
            pltpu.VMEM((rows, features), BF16),
            pltpu.VMEM((features, columns), BF16),
            pltpu.VMEM((features, 128), F32),
            pltpu.VMEM((features, HEAD), BF16),
            pltpu.VMEM((rows, 128), F32),
            pltpu.VMEM((tp * pieces, 2, half, rows), F32),
            pltpu.VMEM((tp * pieces, 2, half, rows), BF16),
            pltpu.VMEM((tp * pieces, 2, half, rows), BF16),
            pltpu.VMEM((tp * pieces, 2, half, rows), BF16),
            pltpu.VMEM((tp, 8, rows), F32),
            pltpu.VMEM((rows, dp * cap), BF16),
            pltpu.VMEM((SPLIT, half, rows), F32),
            pltpu.VMEM((SPLIT, half, rows), F32),
            pltpu.VMEM((1, rows), F32),
            pltpu.VMEM((pieces, 2, half, dp * cap), BF16),
            dma((tp,)), dma((tp,)), dma((tp * pieces,)), dma((tp * pieces,)), dma((tp * pieces,)),
            dma((pieces, dp)), dma((pieces, dp)), dma((pieces,)), dma((1,)), dma((tp,)),
        ],
        compiler_params=pltpu.CompilerParams(
            collective_id=0, has_side_effects=True, vmem_limit_bytes=56 * 1024 * 1024
        ),
    )(hidden, norm_gain.reshape(features // 128, 128), kv_weight, owners.reshape(1, rows), offsets.reshape(1, rows), jnp.asarray(inverse))
    result = result.reshape(share, dp * cap)
    if direct:
        return result
    received = lax.all_to_all(
        result.reshape(share, dp, cap), "dp", split_axis=1, concat_axis=1, tiled=True
    )
    return received.reshape(share, dp * cap)


def solution(mesh):
    in_specs = (P("dp", "tp"), P("tp"), P("tp", None), P("dp", None), P("dp"))
    out_specs = P("tp", "dp")
    return jax.shard_map(
        per_device, mesh=mesh, in_specs=in_specs, out_specs=out_specs, check_vma=False
    )
```

```python
import functools

import jax
import jax.numpy as jnp
import numpy as np
from jax import lax
from jax.experimental import pallas as pl
from jax.experimental.pallas import tpu as pltpu
from jax.sharding import PartitionSpec as P

HEAD = 128
EPSILON = 1e-05
ROPE_BASE = 500000.0
MESH = pl.DeviceIdType.MESH
SPLIT = 2
LAG = 4
F32 = jnp.float32
BF16 = jnp.bfloat16
EXACT = lax.Precision.HIGHEST


def to_columns(rows):
    weight = jnp.full((rows.shape[0], 128), 0.125, F32)
    return lax.dot_general(
        rows, weight, (((0,), (0,)), ((), ())), precision=EXACT, preferred_element_type=F32
    )


def kernel(
    tp, dp, chunks, cap, key_heads, direct,
    h_hbm, g_ref, w_hbm, owner_ref, offset_ref, inverse_ref, out_ref,
    h_ref, w_ref, gain, scaled, squares, part, sendbuf, from_left, from_right, totals, places,
    cosine, sine, scale, outgoing,
    total_send, total_recv, send_sem, left_recv, right_recv, out_send, out_recv, own_sem, h_sem, w_sem,
):
    z = lax.axis_index("tp")
    group = lax.axis_index("dp")
    rows, features = h_ref.shape
    width = chunks * HEAD
    half = HEAD // 2 // SPLIT
    slots = dp * cap
    pieces = chunks * SPLIT
    edge = (z == 0) | (z == tp - 1)

    barrier = pltpu.get_barrier_semaphore()
    for r in range(1, tp):
        pl.semaphore_signal(barrier, inc=1, device_id={"tp": lax.rem(z + r, tp)}, device_id_type=MESH)
    if direct:
        for r in range(1, dp):
            pl.semaphore_signal(barrier, inc=1, device_id={"dp": lax.rem(group + r, dp)}, device_id_type=MESH)

    def h_copy():
        return pltpu.make_async_copy(h_hbm, h_ref, h_sem.at[0])

    def w_copy(turn):
        dest = jnp.where(z == tp - 1, turn, tp - 1 - turn)
        at = pl.ds(pl.multiple_of(dest * width, HEAD), width)
        return pltpu.make_async_copy(w_hbm.at[:, at], w_ref.at[:, at], w_sem.at[turn])

    w_copy(0).start()
    h_copy().start()
    for turn in range(1, tp):
        w_copy(turn).start()

    for i in range(features // 128):
        gain[i * 128:(i + 1) * 128, :] = to_columns(jnp.broadcast_to(g_ref[i:i + 1, :], (8, 128)))

    def to_right(index):
        return pltpu.make_async_remote_copy(
            src_ref=sendbuf.at[index], dst_ref=from_left.at[index],
            send_sem=send_sem.at[index], recv_sem=left_recv.at[index],
            device_id={"tp": jnp.minimum(z + 1, tp - 1)}, device_id_type=MESH,
        )

    def to_left(index):
        return pltpu.make_async_remote_copy(
            src_ref=sendbuf.at[index], dst_ref=from_right.at[index],
            send_sem=send_sem.at[index], recv_sem=right_recv.at[index],
            device_id={"tp": jnp.maximum(z - 1, 0)}, device_id_type=MESH,
        )

    hops = tp - 1
    stream = hops * pieces
    others = max(hops - 1, 1)
    span = pieces + (pieces + others - 1) * others

    def distance(n):
        return jnp.where(n < pieces, 0, 1 + lax.rem(jnp.maximum(n - pieces, 0), others))

    def piece_of(n):
        m = jnp.maximum(n - pieces, 0)
        return jnp.where(n < pieces, n, m // others - lax.rem(m, others))

    def in_stream(n):
        return (n >= 0) & (n < span) & (piece_of(n) >= 0) & (piece_of(n) < pieces)

    def right_piece(n):
        return (hops - distance(n)) * pieces + piece_of(n)

    def left_piece(n):
        return distance(n) * pieces + piece_of(n)

    tile = rows // 2

    def scale_weights(turn, k):
        dest = jnp.where(z == tp - 1, turn, tp - 1 - turn)
        columns = pl.ds(pl.multiple_of(dest * width + k * HEAD, HEAD), HEAD)
        scaled[...] = (w_ref[:, columns].astype(F32) * gain[...]).astype(BF16)

    def multiply(turn, k):
        dest = jnp.where(z == tp - 1, turn, tp - 1 - turn)
        for first in range(0, rows, tile):
            term = jnp.dot(h_ref[first:first + tile, :], scaled[...], preferred_element_type=F32).T
            for q in range(SPLIT):
                index = (dest * chunks + k) * SPLIT + q
                for side in range(2):
                    piece = term[side * (HEAD // 2) + q * half:side * (HEAD // 2) + (q + 1) * half, :]
                    part[index, side, :, first:first + tile] = piece
                    sendbuf[index, side, :, first:first + tile] = piece.astype(BF16)

    def start_pieces(turn, k):
        for q in range(SPLIT):
            @pl.when(z == 0)
            def _():
                to_right((hops - turn) * pieces + k * SPLIT + q).start()

            @pl.when(z == tp - 1)
            def _():
                to_left(turn * pieces + k * SPLIT + q).start()

    w_copy(0).wait()
    scale_weights(0, 0)
    h_copy().wait()
    multiply(0, 0)
    pl.semaphore_wait(barrier, tp - 1 + (dp - 1 if direct else 0))
    start_pieces(0, 0)

    @pl.loop(1, chunks + hops - 1)
    def _(item):
        turn = jnp.maximum(item - chunks + 1, 0)
        k = jnp.where(item < chunks, item, 0)

        @pl.when(item >= chunks)
        def _():
            w_copy(turn).wait()

        scale_weights(turn, k)
        multiply(turn, k)
        start_pieces(turn, k)

    w_copy(hops).wait()

    def add_squares(step, carry):
        at = pl.ds(pl.multiple_of(step * 32, 32), 32)
        total = jnp.zeros((32, 128), F32)
        for lane in range(0, features, 128):
            wide = h_ref[at, lane:lane + 128].astype(F32)
            total = total + wide * wide
        squares[at, :] = total
        return carry

    lax.fori_loop(0, rows // 32, add_squares, 0, unroll=4)
    totals[z] = lax.dot_general(
        jnp.ones((8, 128), F32), squares[...], (((1,), (1,)), ((), ())),
        precision=EXACT, preferred_element_type=F32,
    )
    total_copies = []
    for r in range(1, tp):
        copy = pltpu.make_async_remote_copy(
            src_ref=totals.at[z], dst_ref=totals.at[z],
            send_sem=total_send.at[r], recv_sem=total_recv.at[r],
            device_id={"tp": lax.rem(z + r, tp)}, device_id_type=MESH,
        )
        copy.start()
        total_copies.append(copy)

    def out_copy(index, r, sender, target):
        return pltpu.make_async_remote_copy(
            src_ref=outgoing.at[index, :, :, pl.ds(pl.multiple_of(target * cap, cap), cap)],
            dst_ref=out_ref.at[index // SPLIT, :, lax.rem(index, SPLIT), :, pl.ds(pl.multiple_of(sender * cap, cap), cap)],
            send_sem=out_send.at[index, r], recv_sem=out_recv.at[index, r],
            device_id={"dp": target}, device_id_type=MESH,
        )

    def own_copy(index):
        home = out_ref.at[index // SPLIT, :, lax.rem(index, SPLIT)]
        if not direct:
            return pltpu.make_async_copy(outgoing.at[index], home, own_sem.at[index])
        at = pl.ds(pl.multiple_of(group * cap, cap), cap)
        return pltpu.make_async_copy(
            outgoing.at[index, :, :, at],
            out_ref.at[index // SPLIT, :, lax.rem(index, SPLIT), :, at], own_sem.at[index],
        )

    def prepare():
        owner = to_columns(jnp.broadcast_to(owner_ref[...].astype(F32), (8, rows)))
        lane = lax.broadcasted_iota(jnp.int32, (1, 128), 1).astype(F32)
        named = jnp.where(owner == lane, 1.0, 0.0)
        earlier = jnp.where(
            lax.broadcasted_iota(jnp.int32, (rows, rows), 0) > lax.broadcasted_iota(jnp.int32, (rows, rows), 1),
            1.0, 0.0,
        ).astype(BF16)
        before = jnp.dot(earlier, named.astype(BF16), preferred_element_type=F32)
        rank = jnp.sum(before * named, axis=1, keepdims=True)
        slot = owner[:, 0:1] * cap + rank
        for first in range(0, slots, 256):
            here = (lax.broadcasted_iota(jnp.int32, (1, 256), 1) + first).astype(F32)
            places[:, first:first + 256] = jnp.where(slot == here, 1.0, 0.0).astype(BF16)
        offset = offset_ref[...].astype(F32)
        for q in range(SPLIT):
            angle = inverse_ref[q * half:(q + 1) * half, 0:1] * offset
            cosine[q] = jnp.cos(angle)
            sine[q] = jnp.sin(angle)

        for r in range(1, tp):
            total_copies[r - 1].wait()
        total = totals[0]
        for other in range(1, tp):
            total = total + totals[other]
        scale[...] = lax.rsqrt(total[0:1, :] / (features * tp) + EPSILON)

    final_at = jnp.where(
        edge, 2 * stream // 3, pieces + jnp.maximum(
            (hops - 1 - z) * (others + 1) + LAG * z, (z - 1) * (others + 1) + LAG * (hops - z)
        )
    )
    stride = jnp.where(edge, 1, others)
    steps = span + (LAG + 1) * hops + pieces * others

    @pl.loop(0, steps)
    def _(step):
        @pl.when(step == 0)
        def _():
            @pl.loop(0, chunks)
            def _(k):
                scale_weights(hops, k)
                multiply(hops, k)

        @pl.when(step == jnp.where(edge, 0, pieces))
        def _():
            @pl.loop(0, (chunks - 1) * (hops - 1))
            def _(item):
                k = 1 + item // others
                turn = 1 + lax.rem(item, others)
                scale_weights(turn, k)
                multiply(turn, k)

        @pl.when(step == jnp.where(edge, 0, pieces + 4))
        def _():
            prepare()

        from_left_n = step - LAG * z
        from_right_n = step - LAG * (hops - z)

        @pl.when((z > 0) & in_stream(from_left_n) & (hops - distance(from_left_n) > z))
        def _():
            index = right_piece(from_left_n)
            to_right(index).wait_recv()
            sendbuf[index] = (part[index] + from_left[index].astype(F32)).astype(BF16)
            to_right(index).start()

        @pl.when((z < hops) & in_stream(from_right_n) & (distance(from_right_n) < z))
        def _():
            index = left_piece(from_right_n)
            to_left(index).wait_recv()
            sendbuf[index] = (part[index] + from_right[index].astype(F32)).astype(BF16)
            to_left(index).start()

        later = in_stream(step) & (step >= pieces) & (piece_of(step) >= SPLIT)

        @pl.when((z == 0) & in_stream(step - 2))
        def _():
            to_right(right_piece(step - 2)).wait_send()

        @pl.when((z == 0) & later)
        def _():
            to_right(right_piece(step)).start()

        @pl.when((z == hops) & in_stream(step - 2))
        def _():
            to_left(left_piece(step - 2)).wait_send()

        @pl.when((z == hops) & later)
        def _():
            to_left(left_piece(step)).start()

        def finish(place):
            index = z * pieces + place
            q = lax.rem(place, SPLIT)

            @pl.when(z < tp - 1)
            def _():
                to_left(index).wait_recv()
                part[index] = part[index] + from_right[index].astype(F32)

            @pl.when(z > 0)
            def _():
                to_right(index).wait_recv()
                part[index] = part[index] + from_left[index].astype(F32)

            first = part[index, 0] * scale[...]
            second = part[index, 1] * scale[...]
            is_key = index // SPLIT < key_heads
            cos, sin = cosine[q], sine[q]
            turned = jnp.concatenate(
                [
                    jnp.where(is_key, first * cos - second * sin, first).astype(BF16),
                    jnp.where(is_key, second * cos + first * sin, second).astype(BF16),
                ],
                axis=0,
            )
            if direct:
                for r in range(1, dp + 1):
                    target = lax.rem(group + r, dp)
                    at = pl.ds(pl.multiple_of(target * cap, cap), cap)
                    outgoing[place, :, :, at] = jnp.dot(
                        turned, places[:, at], preferred_element_type=F32
                    ).astype(BF16).reshape(2, half, cap)
                    if r < dp:
                        out_copy(place, r, group, target).start()
            else:
                outgoing[place] = jnp.dot(
                    turned, places[...], preferred_element_type=F32
                ).astype(BF16).reshape(2, half, slots)
            own_copy(place).start()

        since = jnp.maximum(step - final_at, 0)

        @pl.when((step >= final_at) & (since < pieces * stride) & (lax.rem(since, stride) == 0))
        def _():
            finish(jnp.where(edge, since, since // others))

    @pl.loop(0, tp * pieces)
    def _(index):
        dest = index // pieces

        @pl.when((dest > z) & (z > 0))
        def _():
            to_right(index).wait_send()

        @pl.when((dest < z) & (z < hops))
        def _():
            to_left(index).wait_send()

    @pl.loop(0, pieces)
    def _(place):
        own_copy(place).wait()
        if direct:
            for r in range(1, dp):
                out_copy(place, r, group, lax.rem(group + r, dp)).wait_send()
                out_copy(place, r, lax.rem(group + dp - r, dp), group).wait_recv()


def per_device(hidden, norm_gain, kv_weight, owners, offsets):
    dp, tp = lax.axis_size("dp"), lax.axis_size("tp")
    rows, features = hidden.shape
    cap = 2 * rows // dp
    columns = kv_weight.shape[1]
    share = columns // tp
    chunks = share // HEAD
    direct = cap % 128 == 0
    exponent = np.arange(HEAD // 2) * (2.0 / HEAD)
    inverse = np.repeat((ROPE_BASE ** (-exponent)).astype(np.float32)[:, None], 128, axis=1)
    vmem = pl.BlockSpec(memory_space=pltpu.VMEM)
    hbm = pl.BlockSpec(memory_space=pl.ANY)
    pieces = chunks * SPLIT
    half = HEAD // 2 // SPLIT
    dma = pltpu.SemaphoreType.DMA
    result = pl.pallas_call(
        functools.partial(kernel, tp, dp, chunks, cap, columns // (2 * HEAD), direct),
        out_shape=jax.ShapeDtypeStruct((chunks, 2, SPLIT, half, dp * cap), BF16),
        in_specs=[hbm, vmem, hbm, vmem, vmem, vmem],
        out_specs=hbm,
        scratch_shapes=[
            pltpu.VMEM((rows, features), BF16),
            pltpu.VMEM((features, columns), BF16),
            pltpu.VMEM((features, 128), F32),
            pltpu.VMEM((features, HEAD), BF16),
            pltpu.VMEM((rows, 128), F32),
            pltpu.VMEM((tp * pieces, 2, half, rows), F32),
            pltpu.VMEM((tp * pieces, 2, half, rows), BF16),
            pltpu.VMEM((tp * pieces, 2, half, rows), BF16),
            pltpu.VMEM((tp * pieces, 2, half, rows), BF16),
            pltpu.VMEM((tp, 8, rows), F32),
            pltpu.VMEM((rows, dp * cap), BF16),
            pltpu.VMEM((SPLIT, half, rows), F32),
            pltpu.VMEM((SPLIT, half, rows), F32),
            pltpu.VMEM((1, rows), F32),
            pltpu.VMEM((pieces, 2, half, dp * cap), BF16),
            dma((tp,)), dma((tp,)), dma((tp * pieces,)), dma((tp * pieces,)), dma((tp * pieces,)),
            dma((pieces, dp)), dma((pieces, dp)), dma((pieces,)), dma((1,)), dma((tp,)),
        ],
        compiler_params=pltpu.CompilerParams(
            collective_id=0, has_side_effects=True, vmem_limit_bytes=56 * 1024 * 1024
        ),
    )(hidden, norm_gain.reshape(features // 128, 128), kv_weight, owners.reshape(1, rows), offsets.reshape(1, rows), jnp.asarray(inverse))
    result = result.reshape(share, dp * cap)
    if direct:
        return result
    received = lax.all_to_all(
        result.reshape(share, dp, cap), "dp", split_axis=1, concat_axis=1, tiled=True
    )
    return received.reshape(share, dp * cap)


def solution(mesh):
    in_specs = (P("dp", "tp"), P("tp"), P("tp", None), P("dp", None), P("dp"))
    out_specs = P("tp", "dp")
    return jax.shard_map(
        per_device, mesh=mesh, in_specs=in_specs, out_specs=out_specs, check_vma=False
    )
```

```python
import functools

import jax
import jax.numpy as jnp
import numpy as np
from jax import lax
from jax.experimental import pallas as pl
from jax.experimental.pallas import tpu as pltpu
from jax.sharding import PartitionSpec as P

HEAD = 128
EPSILON = 1e-05
ROPE_BASE = 500000.0
MESH = pl.DeviceIdType.MESH
SPLIT = 2
LAG = 4
F32 = jnp.float32
BF16 = jnp.bfloat16
EXACT = lax.Precision.HIGHEST


def to_columns(rows):
    weight = jnp.full((rows.shape[0], 128), 0.125, F32)
    return lax.dot_general(
        rows, weight, (((0,), (0,)), ((), ())), precision=EXACT, preferred_element_type=F32
    )


def kernel(
    tp, dp, chunks, cap, key_heads, direct,
    h_hbm, g_ref, w_hbm, owner_ref, offset_ref, inverse_ref, out_ref,
    h_ref, w_ref, gain, scaled, squares, part, sendbuf, from_left, from_right, totals, places,
    cosine, sine, scale, outgoing,
    total_send, total_recv, send_sem, left_recv, right_recv, out_send, out_recv, own_sem, h_sem, w_sem,
):
    z = lax.axis_index("tp")
    group = lax.axis_index("dp")
    rows, features = h_ref.shape
    width = chunks * HEAD
    half = HEAD // 2 // SPLIT
    slots = dp * cap
    pieces = chunks * SPLIT
    edge = (z == 0) | (z == tp - 1)

    barrier = pltpu.get_barrier_semaphore()
    for r in range(1, tp):
        pl.semaphore_signal(barrier, inc=1, device_id={"tp": lax.rem(z + r, tp)}, device_id_type=MESH)
    if direct:
        for r in range(1, dp):
            pl.semaphore_signal(barrier, inc=1, device_id={"dp": lax.rem(group + r, dp)}, device_id_type=MESH)

    def h_copy():
        return pltpu.make_async_copy(h_hbm, h_ref, h_sem.at[0])

    def w_copy(turn):
        dest = jnp.where(z == tp - 1, turn, tp - 1 - turn)
        at = pl.ds(pl.multiple_of(dest * width, HEAD), width)
        return pltpu.make_async_copy(w_hbm.at[:, at], w_ref.at[:, at], w_sem.at[turn])

    w_copy(0).start()
    h_copy().start()
    for turn in range(1, tp):
        w_copy(turn).start()

    for i in range(features // 128):
        gain[i * 128:(i + 1) * 128, :] = to_columns(jnp.broadcast_to(g_ref[i:i + 1, :], (8, 128)))

    def to_right(index):
        return pltpu.make_async_remote_copy(
            src_ref=sendbuf.at[index], dst_ref=from_left.at[index],
            send_sem=send_sem.at[index], recv_sem=left_recv.at[index],
            device_id={"tp": jnp.minimum(z + 1, tp - 1)}, device_id_type=MESH,
        )

    def to_left(index):
        return pltpu.make_async_remote_copy(
            src_ref=sendbuf.at[index], dst_ref=from_right.at[index],
            send_sem=send_sem.at[index], recv_sem=right_recv.at[index],
            device_id={"tp": jnp.maximum(z - 1, 0)}, device_id_type=MESH,
        )

    hops = tp - 1
    stream = hops * pieces
    others = max(hops - 1, 1)
    span = pieces + (pieces + others - 1) * others

    def distance(n):
        return jnp.where(n < pieces, 0, 1 + lax.rem(jnp.maximum(n - pieces, 0), others))

    def piece_of(n):
        m = jnp.maximum(n - pieces, 0)
        return jnp.where(n < pieces, n, m // others - lax.rem(m, others))

    def in_stream(n):
        return (n >= 0) & (n < span) & (piece_of(n) >= 0) & (piece_of(n) < pieces)

    def right_piece(n):
        return (hops - distance(n)) * pieces + piece_of(n)

    def left_piece(n):
        return distance(n) * pieces + piece_of(n)

    tile = rows // 2

    def scale_weights(turn, k):
        dest = jnp.where(z == tp - 1, turn, tp - 1 - turn)
        columns = pl.ds(pl.multiple_of(dest * width + k * HEAD, HEAD), HEAD)
        scaled[...] = (w_ref[:, columns].astype(F32) * gain[...]).astype(BF16)

    def multiply(turn, k):
        dest = jnp.where(z == tp - 1, turn, tp - 1 - turn)
        for first in range(0, rows, tile):
            term = jnp.dot(h_ref[first:first + tile, :], scaled[...], preferred_element_type=F32).T
            for q in range(SPLIT):
                index = (dest * chunks + k) * SPLIT + q
                for side in range(2):
                    piece = term[side * (HEAD // 2) + q * half:side * (HEAD // 2) + (q + 1) * half, :]
                    part[index, side, :, first:first + tile] = piece
                    sendbuf[index, side, :, first:first + tile] = piece.astype(BF16)

    def start_pieces(turn, k):
        for q in range(SPLIT):
            @pl.when(z == 0)
            def _():
                to_right((hops - turn) * pieces + k * SPLIT + q).start()

            @pl.when(z == tp - 1)
            def _():
                to_left(turn * pieces + k * SPLIT + q).start()

    w_copy(0).wait()
    scale_weights(0, 0)
    h_copy().wait()
    multiply(0, 0)
    pl.semaphore_wait(barrier, tp - 1 + (dp - 1 if direct else 0))
    start_pieces(0, 0)

    @pl.loop(1, chunks + hops - 1)
    def _(item):
        turn = jnp.maximum(item - chunks + 1, 0)
        k = jnp.where(item < chunks, item, 0)

        @pl.when(item >= chunks)
        def _():
            w_copy(turn).wait()

        scale_weights(turn, k)
        multiply(turn, k)
        start_pieces(turn, k)

    w_copy(hops).wait()

    def add_squares(step, carry):
        at = pl.ds(pl.multiple_of(step * 32, 32), 32)
        total = jnp.zeros((32, 128), F32)
        for lane in range(0, features, 128):
            wide = h_ref[at, lane:lane + 128].astype(F32)
            total = total + wide * wide
        squares[at, :] = total
        return carry

    lax.fori_loop(0, rows // 32, add_squares, 0, unroll=4)
    totals[z] = lax.dot_general(
        jnp.ones((8, 128), F32), squares[...], (((1,), (1,)), ((), ())),
        precision=EXACT, preferred_element_type=F32,
    )
    total_copies = []
    for r in range(1, tp):
        copy = pltpu.make_async_remote_copy(
            src_ref=totals.at[z], dst_ref=totals.at[z],
            send_sem=total_send.at[r], recv_sem=total_recv.at[r],
            device_id={"tp": lax.rem(z + r, tp)}, device_id_type=MESH,
        )
        copy.start()
        total_copies.append(copy)

    def out_copy(index, r, sender, target):
        return pltpu.make_async_remote_copy(
            src_ref=outgoing.at[index, :, :, pl.ds(pl.multiple_of(target * cap, cap), cap)],
            dst_ref=out_ref.at[index // SPLIT, :, lax.rem(index, SPLIT), :, pl.ds(pl.multiple_of(sender * cap, cap), cap)],
            send_sem=out_send.at[index, r], recv_sem=out_recv.at[index, r],
            device_id={"dp": target}, device_id_type=MESH,
        )

    def own_copy(index):
        home = out_ref.at[index // SPLIT, :, lax.rem(index, SPLIT)]
        if not direct:
            return pltpu.make_async_copy(outgoing.at[index], home, own_sem.at[index])
        at = pl.ds(pl.multiple_of(group * cap, cap), cap)
        return pltpu.make_async_copy(
            outgoing.at[index, :, :, at],
            out_ref.at[index // SPLIT, :, lax.rem(index, SPLIT), :, at], own_sem.at[index],
        )

    def prepare():
        owner = to_columns(jnp.broadcast_to(owner_ref[...].astype(F32), (8, rows)))
        lane = lax.broadcasted_iota(jnp.int32, (1, 128), 1).astype(F32)
        named = jnp.where(owner == lane, 1.0, 0.0)
        earlier = jnp.where(
            lax.broadcasted_iota(jnp.int32, (rows, rows), 0) > lax.broadcasted_iota(jnp.int32, (rows, rows), 1),
            1.0, 0.0,
        ).astype(BF16)
        before = jnp.dot(earlier, named.astype(BF16), preferred_element_type=F32)
        rank = jnp.sum(before * named, axis=1, keepdims=True)
        slot = owner[:, 0:1] * cap + rank
        for first in range(0, slots, 256):
            here = (lax.broadcasted_iota(jnp.int32, (1, 256), 1) + first).astype(F32)
            places[:, first:first + 256] = jnp.where(slot == here, 1.0, 0.0).astype(BF16)
        offset = offset_ref[...].astype(F32)
        for q in range(SPLIT):
            angle = inverse_ref[q * half:(q + 1) * half, 0:1] * offset
            cosine[q] = jnp.cos(angle)
            sine[q] = jnp.sin(angle)

        for r in range(1, tp):
            total_copies[r - 1].wait()
        total = totals[0]
        for other in range(1, tp):
            total = total + totals[other]
        scale[...] = lax.rsqrt(total[0:1, :] / (features * tp) + EPSILON)

    final_at = jnp.where(
        edge, 2 * stream // 3, pieces + jnp.maximum(
            (hops - 1 - z) * (others + 1) + LAG * z, (z - 1) * (others + 1) + LAG * (hops - z)
        )
    )
    early = min(chunks, 2)
    stride = jnp.where(edge, 1, others)
    steps = span + (LAG + 1) * hops + pieces * others

    @pl.loop(0, steps)
    def _(step):
        @pl.when(step == jnp.where(edge, 0, pieces))
        def _():
            @pl.loop(0, (chunks - 1) * (hops - 1))
            def _(item):
                k = 1 + item // others
                turn = 1 + lax.rem(item, others)
                scale_weights(turn, k)
                multiply(turn, k)

                @pl.when(k < early)
                def _():
                    start_pieces(turn, k)

        @pl.when(step == 0)
        def _():
            @pl.loop(0, chunks)
            def _(k):
                scale_weights(hops, k)
                multiply(hops, k)

        @pl.when(step == jnp.where(edge, 0, pieces + 4))
        def _():
            prepare()

        from_left_n = step - LAG * z
        from_right_n = step - LAG * (hops - z)

        @pl.when((z > 0) & in_stream(from_left_n) & (hops - distance(from_left_n) > z))
        def _():
            index = right_piece(from_left_n)
            to_right(index).wait_recv()
            sendbuf[index] = (part[index] + from_left[index].astype(F32)).astype(BF16)
            to_right(index).start()

        @pl.when((z < hops) & in_stream(from_right_n) & (distance(from_right_n) < z))
        def _():
            index = left_piece(from_right_n)
            to_left(index).wait_recv()
            sendbuf[index] = (part[index] + from_right[index].astype(F32)).astype(BF16)
            to_left(index).start()

        later = in_stream(step) & (step >= pieces) & (piece_of(step) >= early * SPLIT)

        @pl.when((z == 0) & in_stream(step - 2))
        def _():
            to_right(right_piece(step - 2)).wait_send()

        @pl.when((z == 0) & later)
        def _():
            to_right(right_piece(step)).start()

        @pl.when((z == hops) & in_stream(step - 2))
        def _():
            to_left(left_piece(step - 2)).wait_send()

        @pl.when((z == hops) & later)
        def _():
            to_left(left_piece(step)).start()

        def finish(place):
            index = z * pieces + place
            q = lax.rem(place, SPLIT)

            @pl.when(z < tp - 1)
            def _():
                to_left(index).wait_recv()
                part[index] = part[index] + from_right[index].astype(F32)

            @pl.when(z > 0)
            def _():
                to_right(index).wait_recv()
                part[index] = part[index] + from_left[index].astype(F32)

            first = part[index, 0] * scale[...]
            second = part[index, 1] * scale[...]
            is_key = index // SPLIT < key_heads
            cos, sin = cosine[q], sine[q]
            turned = jnp.concatenate(
                [
                    jnp.where(is_key, first * cos - second * sin, first).astype(BF16),
                    jnp.where(is_key, second * cos + first * sin, second).astype(BF16),
                ],
                axis=0,
            )
            if direct:
                for r in range(1, dp + 1):
                    target = lax.rem(group + r, dp)
                    at = pl.ds(pl.multiple_of(target * cap, cap), cap)
                    outgoing[place, :, :, at] = jnp.dot(
                        turned, places[:, at], preferred_element_type=F32
                    ).astype(BF16).reshape(2, half, cap)
                    if r < dp:
                        out_copy(place, r, group, target).start()
            else:
                outgoing[place] = jnp.dot(
                    turned, places[...], preferred_element_type=F32
                ).astype(BF16).reshape(2, half, slots)
            own_copy(place).start()

        since = jnp.maximum(step - final_at, 0)

        @pl.when((step >= final_at) & (since < pieces * stride) & (lax.rem(since, stride) == 0))
        def _():
            finish(jnp.where(edge, since, since // others))

    @pl.loop(0, tp * pieces)
    def _(index):
        dest = index // pieces

        @pl.when((dest > z) & (z > 0))
        def _():
            to_right(index).wait_send()

        @pl.when((dest < z) & (z < hops))
        def _():
            to_left(index).wait_send()

    @pl.loop(0, pieces)
    def _(place):
        own_copy(place).wait()
        if direct:
            for r in range(1, dp):
                out_copy(place, r, group, lax.rem(group + r, dp)).wait_send()
                out_copy(place, r, lax.rem(group + dp - r, dp), group).wait_recv()


def write_out(result_ref, out_ref, sem):
    band = HEAD // 2
    copies = []
    for i in range(out_ref.shape[0] // band):
        at = pl.ds(i * band, band)
        copies.append(pltpu.make_async_copy(result_ref.at[at, :], out_ref.at[at, :], sem.at[i]))
    for copy in copies:
        copy.start()
    for copy in copies:
        copy.wait()


def per_device(hidden, norm_gain, kv_weight, owners, offsets):
    dp, tp = lax.axis_size("dp"), lax.axis_size("tp")
    rows, features = hidden.shape
    cap = 2 * rows // dp
    columns = kv_weight.shape[1]
    share = columns // tp
    chunks = share // HEAD
    direct = cap % 128 == 0
    exponent = np.arange(HEAD // 2) * (2.0 / HEAD)
    inverse = np.repeat((ROPE_BASE ** (-exponent)).astype(np.float32)[:, None], 128, axis=1)
    vmem = pl.BlockSpec(memory_space=pltpu.VMEM)
    hbm = pl.BlockSpec(memory_space=pl.ANY)
    pieces = chunks * SPLIT
    half = HEAD // 2 // SPLIT
    dma = pltpu.SemaphoreType.DMA
    result = pl.pallas_call(
        functools.partial(kernel, tp, dp, chunks, cap, columns // (2 * HEAD), direct),
        out_shape=jax.ShapeDtypeStruct((chunks, 2, SPLIT, half, dp * cap), BF16),
        in_specs=[hbm, vmem, hbm, vmem, vmem, vmem],
        out_specs=hbm,
        scratch_shapes=[
            pltpu.VMEM((rows, features), BF16),
            pltpu.VMEM((features, columns), BF16),
            pltpu.VMEM((features, 128), F32),
            pltpu.VMEM((features, HEAD), BF16),
            pltpu.VMEM((rows, 128), F32),
            pltpu.VMEM((tp * pieces, 2, half, rows), F32),
            pltpu.VMEM((tp * pieces, 2, half, rows), BF16),
            pltpu.VMEM((tp * pieces, 2, half, rows), BF16),
            pltpu.VMEM((tp * pieces, 2, half, rows), BF16),
            pltpu.VMEM((tp, 8, rows), F32),
            pltpu.VMEM((rows, dp * cap), BF16),
            pltpu.VMEM((SPLIT, half, rows), F32),
            pltpu.VMEM((SPLIT, half, rows), F32),
            pltpu.VMEM((1, rows), F32),
            pltpu.VMEM((pieces, 2, half, dp * cap), BF16),
            dma((tp,)), dma((tp,)), dma((tp * pieces,)), dma((tp * pieces,)), dma((tp * pieces,)),
            dma((pieces, dp)), dma((pieces, dp)), dma((pieces,)), dma((1,)), dma((tp,)),
        ],
        compiler_params=pltpu.CompilerParams(
            collective_id=0, has_side_effects=True, vmem_limit_bytes=56 * 1024 * 1024
        ),
    )(hidden, norm_gain.reshape(features // 128, 128), kv_weight, owners.reshape(1, rows), offsets.reshape(1, rows), jnp.asarray(inverse))
    result = result.reshape(share, dp * cap)
    if direct:
        return pl.pallas_call(
            write_out,
            out_shape=jax.ShapeDtypeStruct(result.shape, BF16),
            in_specs=[pl.BlockSpec(memory_space=pltpu.HBM)],
            out_specs=pl.BlockSpec(memory_space=pltpu.HBM),
            scratch_shapes=[dma((share // (HEAD // 2),))],
        )(result)
    received = lax.all_to_all(
        result.reshape(share, dp, cap), "dp", split_axis=1, concat_axis=1, tiled=True
    )
    return received.reshape(share, dp * cap)


def solution(mesh):
    in_specs = (P("dp", "tp"), P("tp"), P("tp", None), P("dp", None), P("dp"))
    out_specs = P("tp", "dp")
    return jax.shard_map(
        per_device, mesh=mesh, in_specs=in_specs, out_specs=out_specs, check_vma=False
    )
```

```python
import functools

import jax
import jax.numpy as jnp
import numpy as np
from jax import lax
from jax.experimental import pallas as pl
from jax.experimental.pallas import tpu as pltpu
from jax.sharding import PartitionSpec as P

HEAD = 128
EPSILON = 1e-05
ROPE_BASE = 500000.0
MESH = pl.DeviceIdType.MESH
SPLIT = 2
LAG = 4
F32 = jnp.float32
BF16 = jnp.bfloat16
EXACT = lax.Precision.HIGHEST


def to_columns(rows):
    weight = jnp.full((rows.shape[0], 128), 0.125, F32)
    return lax.dot_general(
        rows, weight, (((0,), (0,)), ((), ())), precision=EXACT, preferred_element_type=F32
    )


def kernel(
    tp, dp, chunks, cap, key_heads, direct,
    h_hbm, g_ref, w_hbm, owner_ref, offset_ref, inverse_ref, out_ref,
    h_ref, w_ref, gain, scaled, squares, part, sendbuf, from_left, from_right, totals, places,
    cosine, sine, scale, outgoing,
    total_send, total_recv, send_sem, left_recv, right_recv, out_send, out_recv, own_sem, h_sem, w_sem,
):
    z = lax.axis_index("tp")
    group = lax.axis_index("dp")
    rows, features = h_ref.shape
    width = chunks * HEAD
    half = HEAD // 2 // SPLIT
    slots = dp * cap
    pieces = chunks * SPLIT
    edge = (z == 0) | (z == tp - 1)

    barrier = pltpu.get_barrier_semaphore()
    for r in range(1, tp):
        pl.semaphore_signal(barrier, inc=1, device_id={"tp": lax.rem(z + r, tp)}, device_id_type=MESH)
    if direct:
        for r in range(1, dp):
            pl.semaphore_signal(barrier, inc=1, device_id={"dp": lax.rem(group + r, dp)}, device_id_type=MESH)

    def h_copy():
        return pltpu.make_async_copy(h_hbm, h_ref, h_sem.at[0])

    def w_copy(turn):
        dest = jnp.where(z == tp - 1, turn, tp - 1 - turn)
        at = pl.ds(pl.multiple_of(dest * width, HEAD), width)
        return pltpu.make_async_copy(w_hbm.at[:, at], w_ref.at[:, at], w_sem.at[turn])

    w_copy(0).start()
    h_copy().start()
    for turn in range(1, tp):
        w_copy(turn).start()

    for i in range(features // 128):
        gain[i * 128:(i + 1) * 128, :] = to_columns(jnp.broadcast_to(g_ref[i:i + 1, :], (8, 128)))

    def to_right(index):
        return pltpu.make_async_remote_copy(
            src_ref=sendbuf.at[index], dst_ref=from_left.at[index],
            send_sem=send_sem.at[index], recv_sem=left_recv.at[index],
            device_id={"tp": jnp.minimum(z + 1, tp - 1)}, device_id_type=MESH,
        )

    def to_left(index):
        return pltpu.make_async_remote_copy(
            src_ref=sendbuf.at[index], dst_ref=from_right.at[index],
            send_sem=send_sem.at[index], recv_sem=right_recv.at[index],
            device_id={"tp": jnp.maximum(z - 1, 0)}, device_id_type=MESH,
        )

    hops = tp - 1
    stream = hops * pieces
    others = max(hops - 1, 1)
    span = pieces + (pieces + others - 1) * others

    def distance(n):
        return jnp.where(n < pieces, 0, 1 + lax.rem(jnp.maximum(n - pieces, 0), others))

    def piece_of(n):
        m = jnp.maximum(n - pieces, 0)
        return jnp.where(n < pieces, n, m // others - lax.rem(m, others))

    def in_stream(n):
        return (n >= 0) & (n < span) & (piece_of(n) >= 0) & (piece_of(n) < pieces)

    def right_piece(n):
        return (hops - distance(n)) * pieces + piece_of(n)

    def left_piece(n):
        return distance(n) * pieces + piece_of(n)

    tile = rows // 2

    def scale_weights(turn, k):
        dest = jnp.where(z == tp - 1, turn, tp - 1 - turn)
        columns = pl.ds(pl.multiple_of(dest * width + k * HEAD, HEAD), HEAD)
        scaled[...] = (w_ref[:, columns].astype(F32) * gain[...]).astype(BF16)

    def multiply(turn, k):
        dest = jnp.where(z == tp - 1, turn, tp - 1 - turn)
        for first in range(0, rows, tile):
            term = jnp.dot(h_ref[first:first + tile, :], scaled[...], preferred_element_type=F32).T
            for q in range(SPLIT):
                index = (dest * chunks + k) * SPLIT + q
                for side in range(2):
                    piece = term[side * (HEAD // 2) + q * half:side * (HEAD // 2) + (q + 1) * half, :]
                    part[index, side, :, first:first + tile] = piece
                    sendbuf[index, side, :, first:first + tile] = piece.astype(BF16)

    def start_pieces(turn, k):
        for q in range(SPLIT):
            @pl.when(z == 0)
            def _():
                to_right((hops - turn) * pieces + k * SPLIT + q).start()

            @pl.when(z == tp - 1)
            def _():
                to_left(turn * pieces + k * SPLIT + q).start()

    w_copy(0).wait()
    scale_weights(0, 0)
    h_copy().wait()
    multiply(0, 0)
    pl.semaphore_wait(barrier, tp - 1 + (dp - 1 if direct else 0))
    start_pieces(0, 0)

    @pl.loop(1, chunks + hops - 1)
    def _(item):
        turn = jnp.maximum(item - chunks + 1, 0)
        k = jnp.where(item < chunks, item, 0)

        @pl.when(item >= chunks)
        def _():
            w_copy(turn).wait()

        scale_weights(turn, k)
        multiply(turn, k)
        start_pieces(turn, k)

    w_copy(hops).wait()

    def add_squares(step, carry):
        at = pl.ds(pl.multiple_of(step * 32, 32), 32)
        total = jnp.zeros((32, 128), F32)
        for lane in range(0, features, 128):
            wide = h_ref[at, lane:lane + 128].astype(F32)
            total = total + wide * wide
        squares[at, :] = total
        return carry

    lax.fori_loop(0, rows // 32, add_squares, 0, unroll=4)
    totals[z] = lax.dot_general(
        jnp.ones((8, 128), F32), squares[...], (((1,), (1,)), ((), ())),
        precision=EXACT, preferred_element_type=F32,
    )
    total_copies = []
    for r in range(1, tp):
        copy = pltpu.make_async_remote_copy(
            src_ref=totals.at[z], dst_ref=totals.at[z],
            send_sem=total_send.at[r], recv_sem=total_recv.at[r],
            device_id={"tp": lax.rem(z + r, tp)}, device_id_type=MESH,
        )
        copy.start()
        total_copies.append(copy)

    def out_copy(index, r, sender, target):
        return pltpu.make_async_remote_copy(
            src_ref=outgoing.at[index, :, :, pl.ds(pl.multiple_of(target * cap, cap), cap)],
            dst_ref=out_ref.at[index // SPLIT, :, lax.rem(index, SPLIT), :, pl.ds(pl.multiple_of(sender * cap, cap), cap)],
            send_sem=out_send.at[index, r], recv_sem=out_recv.at[index, r],
            device_id={"dp": target}, device_id_type=MESH,
        )

    def own_copy(index):
        home = out_ref.at[index // SPLIT, :, lax.rem(index, SPLIT)]
        if not direct:
            return pltpu.make_async_copy(outgoing.at[index], home, own_sem.at[index])
        at = pl.ds(pl.multiple_of(group * cap, cap), cap)
        return pltpu.make_async_copy(
            outgoing.at[index, :, :, at],
            out_ref.at[index // SPLIT, :, lax.rem(index, SPLIT), :, at], own_sem.at[index],
        )

    def prepare():
        owner = to_columns(jnp.broadcast_to(owner_ref[...].astype(F32), (8, rows)))
        lane = lax.broadcasted_iota(jnp.int32, (1, 128), 1).astype(F32)
        named = jnp.where(owner == lane, 1.0, 0.0)
        earlier = jnp.where(
            lax.broadcasted_iota(jnp.int32, (rows, rows), 0) > lax.broadcasted_iota(jnp.int32, (rows, rows), 1),
            1.0, 0.0,
        ).astype(BF16)
        before = jnp.dot(earlier, named.astype(BF16), preferred_element_type=F32)
        rank = jnp.sum(before * named, axis=1, keepdims=True)
        slot = owner[:, 0:1] * cap + rank
        for first in range(0, slots, 256):
            here = (lax.broadcasted_iota(jnp.int32, (1, 256), 1) + first).astype(F32)
            places[:, first:first + 256] = jnp.where(slot == here, 1.0, 0.0).astype(BF16)
        offset = offset_ref[...].astype(F32)
        for q in range(SPLIT):
            angle = inverse_ref[q * half:(q + 1) * half, 0:1] * offset
            cosine[q] = jnp.cos(angle)
            sine[q] = jnp.sin(angle)

        for r in range(1, tp):
            total_copies[r - 1].wait()
        total = totals[0]
        for other in range(1, tp):
            total = total + totals[other]
        scale[...] = lax.rsqrt(total[0:1, :] / (features * tp) + EPSILON)

    final_at = jnp.where(
        edge, 2 * stream // 3, pieces + jnp.maximum(
            (hops - 1 - z) * (others + 1) + LAG * z, (z - 1) * (others + 1) + LAG * (hops - z)
        )
    )
    early = min(chunks, 2)
    stride = jnp.where(edge, 1, others)
    steps = span + (LAG + 1) * hops + pieces * others

    @pl.loop(0, steps)
    def _(step):
        @pl.when(step == jnp.where(edge, 0, pieces))
        def _():
            @pl.loop(0, (chunks - 1) * (hops - 1))
            def _(item):
                k = 1 + item // others
                turn = 1 + lax.rem(item, others)
                scale_weights(turn, k)
                multiply(turn, k)

                @pl.when(k < early)
                def _():
                    start_pieces(turn, k)

        @pl.when(step == 0)
        def _():
            @pl.loop(0, chunks)
            def _(k):
                scale_weights(hops, k)
                multiply(hops, k)

        @pl.when(step == jnp.where(edge, 0, pieces + 4))
        def _():
            prepare()

        from_left_n = step - LAG * z
        from_right_n = step - LAG * (hops - z)

        @pl.when((z > 0) & in_stream(from_left_n) & (hops - distance(from_left_n) > z))
        def _():
            index = right_piece(from_left_n)
            to_right(index).wait_recv()
            sendbuf[index] = (part[index] + from_left[index].astype(F32)).astype(BF16)
            to_right(index).start()

        @pl.when((z < hops) & in_stream(from_right_n) & (distance(from_right_n) < z))
        def _():
            index = left_piece(from_right_n)
            to_left(index).wait_recv()
            sendbuf[index] = (part[index] + from_right[index].astype(F32)).astype(BF16)
            to_left(index).start()

        later = in_stream(step) & (step >= pieces) & (piece_of(step) >= early * SPLIT)

        @pl.when((z == 0) & in_stream(step - 2))
        def _():
            to_right(right_piece(step - 2)).wait_send()

        @pl.when((z == 0) & later)
        def _():
            to_right(right_piece(step)).start()

        @pl.when((z == hops) & in_stream(step - 2))
        def _():
            to_left(left_piece(step - 2)).wait_send()

        @pl.when((z == hops) & later)
        def _():
            to_left(left_piece(step)).start()

        def finish(place):
            index = z * pieces + place
            q = lax.rem(place, SPLIT)

            @pl.when(z < tp - 1)
            def _():
                to_left(index).wait_recv()
                part[index] = part[index] + from_right[index].astype(F32)

            @pl.when(z > 0)
            def _():
                to_right(index).wait_recv()
                part[index] = part[index] + from_left[index].astype(F32)

            first = part[index, 0] * scale[...]
            second = part[index, 1] * scale[...]
            is_key = index // SPLIT < key_heads
            cos, sin = cosine[q], sine[q]
            turned = jnp.concatenate(
                [
                    jnp.where(is_key, first * cos - second * sin, first).astype(BF16),
                    jnp.where(is_key, second * cos + first * sin, second).astype(BF16),
                ],
                axis=0,
            )
            if direct:
                for r in range(1, dp + 1):
                    target = lax.rem(group + r, dp)
                    at = pl.ds(pl.multiple_of(target * cap, cap), cap)
                    outgoing[place, :, :, at] = jnp.dot(
                        turned, places[:, at], preferred_element_type=F32
                    ).astype(BF16).reshape(2, half, cap)
                    if r < dp:
                        out_copy(place, r, group, target).start()
            else:
                outgoing[place] = jnp.dot(
                    turned, places[...], preferred_element_type=F32
                ).astype(BF16).reshape(2, half, slots)
            own_copy(place).start()

        since = jnp.maximum(step - final_at, 0)

        @pl.when((step >= final_at) & (since < pieces * stride) & (lax.rem(since, stride) == 0))
        def _():
            finish(jnp.where(edge, since, since // others))

    @pl.loop(0, tp * pieces)
    def _(index):
        dest = index // pieces

        @pl.when((dest > z) & (z > 0))
        def _():
            to_right(index).wait_send()

        @pl.when((dest < z) & (z < hops))
        def _():
            to_left(index).wait_send()

    @pl.loop(0, pieces)
    def _(place):
        own_copy(place).wait()
        if direct:
            for r in range(1, dp):
                out_copy(place, r, group, lax.rem(group + r, dp)).wait_send()
                out_copy(place, r, lax.rem(group + dp - r, dp), group).wait_recv()


def write_out(result_ref, out_ref, held, in_sem, out_sem):
    band = HEAD // 2
    bands = [pl.ds(i * band, band) for i in range(out_ref.shape[0] // band)]
    loads = [pltpu.make_async_copy(result_ref.at[at, :], held.at[at, :], in_sem.at[i]) for i, at in enumerate(bands)]
    stores = [pltpu.make_async_copy(held.at[at, :], out_ref.at[at, :], out_sem.at[i]) for i, at in enumerate(bands)]
    for load in loads:
        load.start()
    for load, store in zip(loads, stores):
        load.wait()
        store.start()
    for store in stores:
        store.wait()


def per_device(hidden, norm_gain, kv_weight, owners, offsets):
    dp, tp = lax.axis_size("dp"), lax.axis_size("tp")
    rows, features = hidden.shape
    cap = 2 * rows // dp
    columns = kv_weight.shape[1]
    share = columns // tp
    chunks = share // HEAD
    direct = cap % 128 == 0
    exponent = np.arange(HEAD // 2) * (2.0 / HEAD)
    inverse = np.repeat((ROPE_BASE ** (-exponent)).astype(np.float32)[:, None], 128, axis=1)
    vmem = pl.BlockSpec(memory_space=pltpu.VMEM)
    hbm = pl.BlockSpec(memory_space=pl.ANY)
    pieces = chunks * SPLIT
    half = HEAD // 2 // SPLIT
    dma = pltpu.SemaphoreType.DMA
    result = pl.pallas_call(
        functools.partial(kernel, tp, dp, chunks, cap, columns // (2 * HEAD), direct),
        out_shape=jax.ShapeDtypeStruct((chunks, 2, SPLIT, half, dp * cap), BF16),
        in_specs=[hbm, vmem, hbm, vmem, vmem, vmem],
        out_specs=hbm,
        scratch_shapes=[
            pltpu.VMEM((rows, features), BF16),
            pltpu.VMEM((features, columns), BF16),
            pltpu.VMEM((features, 128), F32),
            pltpu.VMEM((features, HEAD), BF16),
            pltpu.VMEM((rows, 128), F32),
            pltpu.VMEM((tp * pieces, 2, half, rows), F32),
            pltpu.VMEM((tp * pieces, 2, half, rows), BF16),
            pltpu.VMEM((tp * pieces, 2, half, rows), BF16),
            pltpu.VMEM((tp * pieces, 2, half, rows), BF16),
            pltpu.VMEM((tp, 8, rows), F32),
            pltpu.VMEM((rows, dp * cap), BF16),
            pltpu.VMEM((SPLIT, half, rows), F32),
            pltpu.VMEM((SPLIT, half, rows), F32),
            pltpu.VMEM((1, rows), F32),
            pltpu.VMEM((pieces, 2, half, dp * cap), BF16),
            dma((tp,)), dma((tp,)), dma((tp * pieces,)), dma((tp * pieces,)), dma((tp * pieces,)),
            dma((pieces, dp)), dma((pieces, dp)), dma((pieces,)), dma((1,)), dma((tp,)),
        ],
        compiler_params=pltpu.CompilerParams(
            collective_id=0, has_side_effects=True, vmem_limit_bytes=56 * 1024 * 1024
        ),
    )(hidden, norm_gain.reshape(features // 128, 128), kv_weight, owners.reshape(1, rows), offsets.reshape(1, rows), jnp.asarray(inverse))
    result = result.reshape(share, dp * cap)
    if direct:
        return pl.pallas_call(
            write_out,
            out_shape=jax.ShapeDtypeStruct(result.shape, BF16),
            in_specs=[pl.BlockSpec(memory_space=pltpu.HBM)],
            out_specs=pl.BlockSpec(memory_space=pltpu.HBM),
            scratch_shapes=[
                pltpu.VMEM(result.shape, BF16), dma((share // (HEAD // 2),)), dma((share // (HEAD // 2),)),
            ],
            compiler_params=pltpu.CompilerParams(vmem_limit_bytes=56 * 1024 * 1024),
        )(result)
    received = lax.all_to_all(
        result.reshape(share, dp, cap), "dp", split_axis=1, concat_axis=1, tiled=True
    )
    return received.reshape(share, dp * cap)


def solution(mesh):
    in_specs = (P("dp", "tp"), P("tp"), P("tp", None), P("dp", None), P("dp"))
    out_specs = P("tp", "dp")
    return jax.shard_map(
        per_device, mesh=mesh, in_specs=in_specs, out_specs=out_specs, check_vma=False
    )
```

```python
import functools

import jax
import jax.numpy as jnp
import numpy as np
from jax import lax
from jax.experimental import pallas as pl
from jax.experimental.pallas import tpu as pltpu
from jax.sharding import PartitionSpec as P

HEAD = 128
EPSILON = 1e-05
ROPE_BASE = 500000.0
MESH = pl.DeviceIdType.MESH
SPLIT = 2
LAG = 3
F32 = jnp.float32
BF16 = jnp.bfloat16
EXACT = lax.Precision.HIGHEST


def to_columns(rows):
    weight = jnp.full((rows.shape[0], 128), 0.125, F32)
    return lax.dot_general(
        rows, weight, (((0,), (0,)), ((), ())), precision=EXACT, preferred_element_type=F32
    )


def kernel(
    tp, dp, chunks, cap, key_heads, direct,
    h_hbm, g_ref, w_hbm, owner_ref, offset_ref, inverse_ref, out_ref,
    h_ref, w_ref, gain, scaled, squares, part, sendbuf, from_left, from_right, totals, places,
    cosine, sine, scale, outgoing,
    total_send, total_recv, send_sem, left_recv, right_recv, out_send, out_recv, own_sem, h_sem, w_sem,
):
    z = lax.axis_index("tp")
    group = lax.axis_index("dp")
    rows, features = h_ref.shape
    width = chunks * HEAD
    half = HEAD // 2 // SPLIT
    slots = dp * cap
    pieces = chunks * SPLIT
    edge = (z == 0) | (z == tp - 1)

    barrier = pltpu.get_barrier_semaphore()
    for r in range(1, tp):
        pl.semaphore_signal(barrier, inc=1, device_id={"tp": lax.rem(z + r, tp)}, device_id_type=MESH)
    if direct:
        for r in range(1, dp):
            pl.semaphore_signal(barrier, inc=1, device_id={"dp": lax.rem(group + r, dp)}, device_id_type=MESH)

    def h_copy():
        return pltpu.make_async_copy(h_hbm, h_ref, h_sem.at[0])

    def w_copy(turn):
        dest = jnp.where(z == tp - 1, turn, tp - 1 - turn)
        at = pl.ds(pl.multiple_of(dest * width, HEAD), width)
        return pltpu.make_async_copy(w_hbm.at[:, at], w_ref.at[:, at], w_sem.at[turn])

    w_copy(0).start()
    h_copy().start()
    for turn in range(1, tp):
        w_copy(turn).start()

    for i in range(features // 128):
        gain[i * 128:(i + 1) * 128, :] = to_columns(jnp.broadcast_to(g_ref[i:i + 1, :], (8, 128)))

    def to_right(index):
        return pltpu.make_async_remote_copy(
            src_ref=sendbuf.at[index], dst_ref=from_left.at[index],
            send_sem=send_sem.at[index], recv_sem=left_recv.at[index],
            device_id={"tp": jnp.minimum(z + 1, tp - 1)}, device_id_type=MESH,
        )

    def to_left(index):
        return pltpu.make_async_remote_copy(
            src_ref=sendbuf.at[index], dst_ref=from_right.at[index],
            send_sem=send_sem.at[index], recv_sem=right_recv.at[index],
            device_id={"tp": jnp.maximum(z - 1, 0)}, device_id_type=MESH,
        )

    hops = tp - 1
    stream = hops * pieces
    others = max(hops - 1, 1)
    span = pieces + (pieces + others - 1) * others

    def distance(n):
        return jnp.where(n < pieces, 0, 1 + lax.rem(jnp.maximum(n - pieces, 0), others))

    def piece_of(n):
        m = jnp.maximum(n - pieces, 0)
        return jnp.where(n < pieces, n, m // others - lax.rem(m, others))

    def in_stream(n):
        return (n >= 0) & (n < span) & (piece_of(n) >= 0) & (piece_of(n) < pieces)

    def right_piece(n):
        return (hops - distance(n)) * pieces + piece_of(n)

    def left_piece(n):
        return distance(n) * pieces + piece_of(n)

    tile = rows // 2

    def scale_weights(turn, k):
        dest = jnp.where(z == tp - 1, turn, tp - 1 - turn)
        columns = pl.ds(pl.multiple_of(dest * width + k * HEAD, HEAD), HEAD)
        scaled[...] = (w_ref[:, columns].astype(F32) * gain[...]).astype(BF16)

    def multiply(turn, k):
        dest = jnp.where(z == tp - 1, turn, tp - 1 - turn)
        for first in range(0, rows, tile):
            term = jnp.dot(h_ref[first:first + tile, :], scaled[...], preferred_element_type=F32).T
            for q in range(SPLIT):
                index = (dest * chunks + k) * SPLIT + q
                for side in range(2):
                    piece = term[side * (HEAD // 2) + q * half:side * (HEAD // 2) + (q + 1) * half, :]
                    part[index, side, :, first:first + tile] = piece
                    sendbuf[index, side, :, first:first + tile] = piece.astype(BF16)

    def start_pieces(turn, k):
        for q in range(SPLIT):
            @pl.when(z == 0)
            def _():
                to_right((hops - turn) * pieces + k * SPLIT + q).start()

            @pl.when(z == tp - 1)
            def _():
                to_left(turn * pieces + k * SPLIT + q).start()

    w_copy(0).wait()
    scale_weights(0, 0)
    h_copy().wait()
    multiply(0, 0)
    pl.semaphore_wait(barrier, tp - 1 + (dp - 1 if direct else 0))
    start_pieces(0, 0)

    @pl.loop(1, chunks + hops - 1)
    def _(item):
        turn = jnp.maximum(item - chunks + 1, 0)
        k = jnp.where(item < chunks, item, 0)

        @pl.when(item >= chunks)
        def _():
            w_copy(turn).wait()

        scale_weights(turn, k)
        multiply(turn, k)
        start_pieces(turn, k)

    w_copy(hops).wait()

    def add_squares(step, carry):
        at = pl.ds(pl.multiple_of(step * 32, 32), 32)
        total = jnp.zeros((32, 128), F32)
        for lane in range(0, features, 128):
            wide = h_ref[at, lane:lane + 128].astype(F32)
            total = total + wide * wide
        squares[at, :] = total
        return carry

    lax.fori_loop(0, rows // 32, add_squares, 0, unroll=4)
    totals[z] = lax.dot_general(
        jnp.ones((8, 128), F32), squares[...], (((1,), (1,)), ((), ())),
        precision=EXACT, preferred_element_type=F32,
    )
    total_copies = []
    for r in range(1, tp):
        copy = pltpu.make_async_remote_copy(
            src_ref=totals.at[z], dst_ref=totals.at[z],
            send_sem=total_send.at[r], recv_sem=total_recv.at[r],
            device_id={"tp": lax.rem(z + r, tp)}, device_id_type=MESH,
        )
        copy.start()
        total_copies.append(copy)

    def out_copy(index, r, sender, target):
        return pltpu.make_async_remote_copy(
            src_ref=outgoing.at[index, :, :, pl.ds(pl.multiple_of(target * cap, cap), cap)],
            dst_ref=out_ref.at[index // SPLIT, :, lax.rem(index, SPLIT), :, pl.ds(pl.multiple_of(sender * cap, cap), cap)],
            send_sem=out_send.at[index, r], recv_sem=out_recv.at[index, r],
            device_id={"dp": target}, device_id_type=MESH,
        )

    def own_copy(index):
        home = out_ref.at[index // SPLIT, :, lax.rem(index, SPLIT)]
        if not direct:
            return pltpu.make_async_copy(outgoing.at[index], home, own_sem.at[index])
        at = pl.ds(pl.multiple_of(group * cap, cap), cap)
        return pltpu.make_async_copy(
            outgoing.at[index, :, :, at],
            out_ref.at[index // SPLIT, :, lax.rem(index, SPLIT), :, at], own_sem.at[index],
        )

    def prepare():
        owner = to_columns(jnp.broadcast_to(owner_ref[...].astype(F32), (8, rows)))
        lane = lax.broadcasted_iota(jnp.int32, (1, 128), 1).astype(F32)
        named = jnp.where(owner == lane, 1.0, 0.0)
        earlier = jnp.where(
            lax.broadcasted_iota(jnp.int32, (rows, rows), 0) > lax.broadcasted_iota(jnp.int32, (rows, rows), 1),
            1.0, 0.0,
        ).astype(BF16)
        before = jnp.dot(earlier, named.astype(BF16), preferred_element_type=F32)
        rank = jnp.sum(before * named, axis=1, keepdims=True)
        slot = owner[:, 0:1] * cap + rank
        for first in range(0, slots, 256):
            here = (lax.broadcasted_iota(jnp.int32, (1, 256), 1) + first).astype(F32)
            places[:, first:first + 256] = jnp.where(slot == here, 1.0, 0.0).astype(BF16)
        offset = offset_ref[...].astype(F32)
        for q in range(SPLIT):
            angle = inverse_ref[q * half:(q + 1) * half, 0:1] * offset
            cosine[q] = jnp.cos(angle)
            sine[q] = jnp.sin(angle)

        for r in range(1, tp):
            total_copies[r - 1].wait()
        total = totals[0]
        for other in range(1, tp):
            total = total + totals[other]
        scale[...] = lax.rsqrt(total[0:1, :] / (features * tp) + EPSILON)

    final_at = jnp.where(
        edge, 2 * stream // 3, pieces + jnp.maximum(
            (hops - 1 - z) * (others + 1) + LAG * z, (z - 1) * (others + 1) + LAG * (hops - z)
        )
    )
    early = min(chunks, 2)
    stride = jnp.where(edge, 1, others)
    steps = span + (LAG + 1) * hops + pieces * others

    @pl.loop(0, steps)
    def _(step):
        @pl.when(step == jnp.where(edge, 0, pieces))
        def _():
            @pl.loop(0, (chunks - 1) * (hops - 1))
            def _(item):
                k = 1 + item // others
                turn = 1 + lax.rem(item, others)
                scale_weights(turn, k)
                multiply(turn, k)

                @pl.when(k < early)
                def _():
                    start_pieces(turn, k)

        @pl.when(step == 0)
        def _():
            @pl.loop(0, chunks)
            def _(k):
                scale_weights(hops, k)
                multiply(hops, k)

        @pl.when(step == jnp.where(edge, 0, pieces + 4))
        def _():
            prepare()

        from_left_n = step - LAG * z
        from_right_n = step - LAG * (hops - z)

        @pl.when((z > 0) & in_stream(from_left_n) & (hops - distance(from_left_n) > z))
        def _():
            index = right_piece(from_left_n)
            to_right(index).wait_recv()
            sendbuf[index] = (part[index] + from_left[index].astype(F32)).astype(BF16)
            to_right(index).start()

        @pl.when((z < hops) & in_stream(from_right_n) & (distance(from_right_n) < z))
        def _():
            index = left_piece(from_right_n)
            to_left(index).wait_recv()
            sendbuf[index] = (part[index] + from_right[index].astype(F32)).astype(BF16)
            to_left(index).start()

        later = in_stream(step) & (step >= pieces) & (piece_of(step) >= early * SPLIT)

        @pl.when((z == 0) & in_stream(step - 2))
        def _():
            to_right(right_piece(step - 2)).wait_send()

        @pl.when((z == 0) & later)
        def _():
            to_right(right_piece(step)).start()

        @pl.when((z == hops) & in_stream(step - 2))
        def _():
            to_left(left_piece(step - 2)).wait_send()

        @pl.when((z == hops) & later)
        def _():
            to_left(left_piece(step)).start()

        def finish(place):
            index = z * pieces + place
            q = lax.rem(place, SPLIT)

            @pl.when(z < tp - 1)
            def _():
                to_left(index).wait_recv()
                part[index] = part[index] + from_right[index].astype(F32)

            @pl.when(z > 0)
            def _():
                to_right(index).wait_recv()
                part[index] = part[index] + from_left[index].astype(F32)

            first = part[index, 0] * scale[...]
            second = part[index, 1] * scale[...]
            is_key = index // SPLIT < key_heads
            cos, sin = cosine[q], sine[q]
            turned = jnp.concatenate(
                [
                    jnp.where(is_key, first * cos - second * sin, first).astype(BF16),
                    jnp.where(is_key, second * cos + first * sin, second).astype(BF16),
                ],
                axis=0,
            )
            if direct:
                for r in range(1, dp + 1):
                    target = lax.rem(group + r, dp)
                    at = pl.ds(pl.multiple_of(target * cap, cap), cap)
                    outgoing[place, :, :, at] = jnp.dot(
                        turned, places[:, at], preferred_element_type=F32
                    ).astype(BF16).reshape(2, half, cap)
                    if r < dp:
                        out_copy(place, r, group, target).start()
            else:
                outgoing[place] = jnp.dot(
                    turned, places[...], preferred_element_type=F32
                ).astype(BF16).reshape(2, half, slots)
            own_copy(place).start()

        since = jnp.maximum(step - final_at, 0)

        @pl.when((step >= final_at) & (since < pieces * stride) & (lax.rem(since, stride) == 0))
        def _():
            finish(jnp.where(edge, since, since // others))

    @pl.loop(0, tp * pieces)
    def _(index):
        dest = index // pieces

        @pl.when((dest > z) & (z > 0))
        def _():
            to_right(index).wait_send()

        @pl.when((dest < z) & (z < hops))
        def _():
            to_left(index).wait_send()

    @pl.loop(0, pieces)
    def _(place):
        own_copy(place).wait()
        if direct:
            for r in range(1, dp):
                out_copy(place, r, group, lax.rem(group + r, dp)).wait_send()
                out_copy(place, r, lax.rem(group + dp - r, dp), group).wait_recv()


def write_out(result_ref, out_ref, held, in_sem, out_sem):
    band = HEAD // 2
    bands = [pl.ds(i * band, band) for i in range(out_ref.shape[0] // band)]
    loads = [pltpu.make_async_copy(result_ref.at[at, :], held.at[at, :], in_sem.at[i]) for i, at in enumerate(bands)]
    stores = [pltpu.make_async_copy(held.at[at, :], out_ref.at[at, :], out_sem.at[i]) for i, at in enumerate(bands)]
    for load in loads:
        load.start()
    for load, store in zip(loads, stores):
        load.wait()
        store.start()
    for store in stores:
        store.wait()


def per_device(hidden, norm_gain, kv_weight, owners, offsets):
    dp, tp = lax.axis_size("dp"), lax.axis_size("tp")
    rows, features = hidden.shape
    cap = 2 * rows // dp
    columns = kv_weight.shape[1]
    share = columns // tp
    chunks = share // HEAD
    direct = cap % 128 == 0
    exponent = np.arange(HEAD // 2) * (2.0 / HEAD)
    inverse = np.repeat((ROPE_BASE ** (-exponent)).astype(np.float32)[:, None], 128, axis=1)
    vmem = pl.BlockSpec(memory_space=pltpu.VMEM)
    hbm = pl.BlockSpec(memory_space=pl.ANY)
    pieces = chunks * SPLIT
    half = HEAD // 2 // SPLIT
    dma = pltpu.SemaphoreType.DMA
    result = pl.pallas_call(
        functools.partial(kernel, tp, dp, chunks, cap, columns // (2 * HEAD), direct),
        out_shape=jax.ShapeDtypeStruct((chunks, 2, SPLIT, half, dp * cap), BF16),
        in_specs=[hbm, vmem, hbm, vmem, vmem, vmem],
        out_specs=hbm,
        scratch_shapes=[
            pltpu.VMEM((rows, features), BF16),
            pltpu.VMEM((features, columns), BF16),
            pltpu.VMEM((features, 128), F32),
            pltpu.VMEM((features, HEAD), BF16),
            pltpu.VMEM((rows, 128), F32),
            pltpu.VMEM((tp * pieces, 2, half, rows), F32),
            pltpu.VMEM((tp * pieces, 2, half, rows), BF16),
            pltpu.VMEM((tp * pieces, 2, half, rows), BF16),
            pltpu.VMEM((tp * pieces, 2, half, rows), BF16),
            pltpu.VMEM((tp, 8, rows), F32),
            pltpu.VMEM((rows, dp * cap), BF16),
            pltpu.VMEM((SPLIT, half, rows), F32),
            pltpu.VMEM((SPLIT, half, rows), F32),
            pltpu.VMEM((1, rows), F32),
            pltpu.VMEM((pieces, 2, half, dp * cap), BF16),
            dma((tp,)), dma((tp,)), dma((tp * pieces,)), dma((tp * pieces,)), dma((tp * pieces,)),
            dma((pieces, dp)), dma((pieces, dp)), dma((pieces,)), dma((1,)), dma((tp,)),
        ],
        compiler_params=pltpu.CompilerParams(
            collective_id=0, has_side_effects=True, vmem_limit_bytes=56 * 1024 * 1024
        ),
    )(hidden, norm_gain.reshape(features // 128, 128), kv_weight, owners.reshape(1, rows), offsets.reshape(1, rows), jnp.asarray(inverse))
    result = result.reshape(share, dp * cap)
    if direct:
        return pl.pallas_call(
            write_out,
            out_shape=jax.ShapeDtypeStruct(result.shape, BF16),
            in_specs=[pl.BlockSpec(memory_space=pltpu.HBM)],
            out_specs=pl.BlockSpec(memory_space=pltpu.HBM),
            scratch_shapes=[
                pltpu.VMEM(result.shape, BF16), dma((share // (HEAD // 2),)), dma((share // (HEAD // 2),)),
            ],
            compiler_params=pltpu.CompilerParams(vmem_limit_bytes=56 * 1024 * 1024),
        )(result)
    received = lax.all_to_all(
        result.reshape(share, dp, cap), "dp", split_axis=1, concat_axis=1, tiled=True
    )
    return received.reshape(share, dp * cap)


def solution(mesh):
    in_specs = (P("dp", "tp"), P("tp"), P("tp", None), P("dp", None), P("dp"))
    out_specs = P("tp", "dp")
    return jax.shard_map(
        per_device, mesh=mesh, in_specs=in_specs, out_specs=out_specs, check_vma=False
    )
```
